1024 devices in a mesh: own: 32 (over z_lo, x, core), grp: 32 (over y, z_hi).
Axes of the slice: x: 4, y: 8, z: 16 (z_hi: 4, z_lo: 4; z = z_hi * 4 + z_lo), core: 2. Of those that a mesh axis runs over, the one named last changes fastest.
Arguments:
- tokens: bfloat16 [4096, 2048], P('own'), may hold values from -6 to 6
- cotangent: bfloat16 [4096, 2048], P('own'), may hold values from -6 to 6
- route_ids: int32 [4096, 6], P('own'), may hold values from 0 to 63, all different within a row; in each aligned block of 128 rows (0 to 127, 128 to 255, ...) at most 15 rows name the same one
- route_weights: float32 [4096, 6], P('own'), may hold values from 0.1 to 1
- gate_weight: bfloat16 [1024, 512, 352], P(('own', 'grp')), may hold values from -0.125 to 0.125
- up_weight: bfloat16 [1024, 512, 352], P(('own', 'grp')), may hold values from -0.125 to 0.125
- down_weight_t: bfloat16 [1024, 512, 352], P(('own', 'grp')), may hold values from -0.15625 to 0.15625
Outputs:
- layer_out: bfloat16 [4096, 2048], P('own', 'grp')
- token_grad: bfloat16 [4096, 2048], P('own', 'grp')
- gate_grad: float32 [1024, 512, 352], P(('own', 'grp'))
- up_grad: float32 [1024, 512, 352], P(('own', 'grp'))
- down_grad: float32 [1024, 512, 352], P(('own', 'grp'))
The draws below stay inside these ranges and needn't reach their ends.
Inputs may be any that keep to these rules, and one draw needn't show every extreme that they name: `route_ids`: each row names 6 different experts. In each aligned block of 128 rows (the rows of one index of own) no expert is named by more than 15 rows, a bound that some block reaches.
All inputs are finite; a program needn't handle non-finite values.
Results may differ from the reference program's by a relative error of at most 0.0064.
Values may be sent and summed in bfloat16 or wider, within the bound.
A program may use at most 32 MiB of HBM per device.

```python
import math
import jax
import jax.numpy as jnp
import numpy as np
from jax import lax

D = 2048
FF = 1408
TOP = 6
EXP_DEV = 2
TOK_DEV = 128
EXPERTS = 64
TOKENS = 4096
DS = 4
FS = 4
DQ = 512
FQ = 352
TILES = 1024
CAP = 15
N_OWN = 32


def steps_of(stream_key, dims, split, smallest, top_value):
    loudness = 1.0
    for position, shards_of in split:
        heights = jax.random.uniform(jax.random.fold_in(jax.random.fold_in(stream_key, 6), position), (shards_of,), jnp.float32, smallest / len(split), top_value / len(split))
        loudness = loudness * jnp.repeat(jnp.exp(heights), dims[position] // shards_of).reshape((-1,) + (1,) * (len(dims) - 1 - position))
    return loudness


def deal_out(stream_key, own, number, rows, count, top, bound, slope):
    ranking = jax.random.permutation(stream_key, count)
    heavy_load, usual = portions_of(count, rows * top, bound, slope, True), portions_of(count, rows * top, bound, slope, False)
    places = jnp.arange(count)

    def named(sizes, rotation):
        used = int((sizes > 0).sum())
        fixed = max(1, used // 4)
        shifted = fixed + (places - fixed + rotation * (used - fixed)) % max(1, count - fixed)
        return jnp.zeros((count,), jnp.int32).at[ranking[jnp.where(places < fixed, places, shifted)]].set(jnp.asarray(sizes, jnp.int32))

    sizes = jnp.where(number % 4 == 0, named(heavy_load, number // 4), named(usual, number - number // 4 - 1))
    mixed = jax.random.permutation(jax.random.fold_in(own, 3), count)
    source_of, taker = mixed[0:count // 2 * 2:2], mixed[1:count // 2 * 2:2]
    margin = jnp.minimum(sizes[source_of] - 1, bound - sizes[taker]) // 2
    margin = jnp.where((source_of == ranking[0]) | (taker == ranking[0]) | (sizes[taker] == 0), 0, jnp.maximum(margin, 0))
    shifted = jax.random.randint(jax.random.fold_in(own, 4), (count // 2,), 0, 1 << 20) % (margin + 1)
    sizes = sizes.at[source_of].add(-shifted).at[taker].add(shifted)
    items = jnp.searchsorted(jnp.cumsum(sizes), jnp.arange(rows * top), side="right").astype(jnp.int32)
    listing = items.reshape(top, rows).T
    listing = listing[jax.random.permutation(jax.random.fold_in(own, 1), rows)]
    rotation = jax.random.randint(jax.random.fold_in(own, 2), (rows, 1), 0, top)
    return jnp.take_along_axis(listing, (jnp.arange(top)[None, :] + rotation) % top, axis=1)


def portions_of(number_of, total, limit, slope, full):
    loads = [(1 << 20) // math.isqrt(standing ** slope) + 1 for standing in range(1, number_of + 1)]
    largest = limit if full else min(limit, max(-(-total // number_of), total * loads[0] // sum(loads)))
    least = 1 if total - largest >= number_of - 1 else 0
    counts, surplus = [largest] + [least] * (number_of - 1), total - largest - least * (number_of - 1)
    while surplus > 0:
        movable = [i for i in range(1, number_of) if counts[i] < largest] or [i for i in range(1, number_of) if counts[i] < limit]
        whole, budget = sum([loads[i] for i in movable]), surplus
        for i in movable:
            addition = min(limit - counts[i], max(1, budget * loads[i] // whole), surplus)
            counts[i] = counts[i] + addition
            surplus = surplus - addition
    return np.array(counts)


def noise(stream_key, dims, deviation, bound, shards=(), held_as=jnp.bfloat16):
    entries = deviation * jax.random.normal(stream_key, dims, jnp.float32)
    if shards:
        entries = entries * steps_of(stream_key, dims, shards, -0.22, 0.18)
    return jnp.clip(entries, -bound, bound).astype(held_as)


def setup_inputs(seed: int = 0) -> dict:
    splits = jax.random.split(jax.random.key(seed), 8)
    tokens = noise(splits[0], (TOKENS, D), 1.0, 6.0, ((0, 32),))
    cotangent = noise(splits[1], (TOKENS, D), 1.0, 6.0, ((0, 32),))
    route_ids_keys = jax.random.split(jax.random.fold_in(splits[2], 1), TOKENS // TOK_DEV)
    route_ids_turns = jax.random.permutation(jax.random.fold_in(splits[2], 3), TOKENS // TOK_DEV)
    route_ids = jax.vmap(lambda own, number: deal_out(jax.random.fold_in(splits[2], 2), own, number, TOK_DEV, EXPERTS, TOP, CAP, 2))(route_ids_keys, route_ids_turns).reshape((TOKENS, TOP))
    route_weights = jnp.clip(jnp.exp(math.log(1.0) - 2.3025851 * jax.random.uniform(splits[3], (TOKENS, TOP), jnp.float32) ** steps_of(splits[3], (TOKENS, TOP), ((0, 32),), -0.2, 0.2)), 0.1, 1.0)
    gate_weight = noise(splits[4], (TILES, DQ, FQ), D ** -0.5, 0.125, ((0, 1024),))
    up_weight = noise(splits[5], (TILES, DQ, FQ), D ** -0.5, 0.125, ((0, 1024),))
    down_weight_t = noise(splits[6], (TILES, DQ, FQ), FF ** -0.5, 0.15625, ((0, 1024),))
    return dict(tokens=tokens, cotangent=cotangent, route_ids=route_ids, route_weights=route_weights, gate_weight=gate_weight, up_weight=up_weight, down_weight_t=down_weight_t)


def to_experts(tiles):
    shaped = tiles.reshape(N_OWN, DS, EXP_DEV, FS, DQ, FQ).transpose(0, 2, 1, 4, 3, 5)
    return shaped.reshape(EXPERTS, D, FF)


def to_tiles(full):
    shaped = full.reshape(N_OWN, EXP_DEV, DS, DQ, FS, FQ).transpose(0, 2, 1, 4, 3, 5)
    return shaped.reshape(TILES, DQ, FQ)


def blocks_rounded(left_side, right_side):
    terms = jnp.einsum("rbf,dbf->rbd", left_side, right_side, precision=lax.Precision.HIGHEST)
    rounded = lax.optimization_barrier(terms.astype(jnp.bfloat16))
    return jnp.sum(rounded.astype(jnp.float32), axis=1)


def expert_pass(operands):
    inputs, cotangents, w_gate, w_up, w_down = operands
    row_count = inputs.shape[0]
    input_wide = inputs.astype(jnp.float32)
    cot_wide = cotangents.astype(jnp.float32)
    gate_full = w_gate.astype(jnp.float32)
    up_full = w_up.astype(jnp.float32)
    down_full = w_down.astype(jnp.float32)
    gating = jnp.einsum("rd,df->rf", input_wide, gate_full, precision=lax.Precision.HIGHEST)
    up_proj = jnp.einsum("rd,df->rf", input_wide, up_full, precision=lax.Precision.HIGHEST)
    grad_hidden = jnp.einsum("rd,df->rf", cot_wide, down_full, precision=lax.Precision.HIGHEST)
    sigmoid_gate = jax.nn.sigmoid(gating)
    hidden = (gating * sigmoid_gate * up_proj).astype(jnp.bfloat16)
    hidden_wide = hidden.astype(jnp.float32)
    grad_gate = (grad_hidden * up_proj * sigmoid_gate * (1.0 + gating * (1.0 - sigmoid_gate))).astype(jnp.bfloat16)
    grad_up = (grad_hidden * gating * sigmoid_gate).astype(jnp.bfloat16)
    gate_wide = grad_gate.astype(jnp.float32)
    upg_wide = grad_up.astype(jnp.float32)
    output = blocks_rounded(hidden_wide.reshape(row_count, FS, FQ), down_full.reshape(D, FS, FQ))
    both_terms = (jnp.einsum("rbf,dbf->rbd", gate_wide.reshape(row_count, FS, FQ), gate_full.reshape(D, FS, FQ),
                             precision=lax.Precision.HIGHEST)
                  + jnp.einsum("rbf,dbf->rbd", upg_wide.reshape(row_count, FS, FQ), up_full.reshape(D, FS, FQ),
                               precision=lax.Precision.HIGHEST))
    rounded_terms = lax.optimization_barrier(both_terms.astype(jnp.bfloat16))
    row_grad = jnp.sum(rounded_terms.astype(jnp.float32), axis=1)
    gate_grad = jnp.einsum("rd,rf->df", input_wide, gate_wide, precision=lax.Precision.HIGHEST)
    up_grad = jnp.einsum("rd,rf->df", input_wide, upg_wide, precision=lax.Precision.HIGHEST)
    down_grad = jnp.einsum("rd,rf->df", cot_wide, hidden_wide, precision=lax.Precision.HIGHEST)
    return output, row_grad, gate_grad, up_grad, down_grad


def reference(tokens, cotangent, route_ids, route_weights, gate_weight, up_weight, down_weight_t):
    row_count = N_OWN * CAP
    flat_ids = route_ids.reshape(N_OWN, TOK_DEV * TOP)
    onehot = (flat_ids[:, :, None] == jnp.arange(EXPERTS, dtype=jnp.int32)[None, None, :]).astype(jnp.int32)
    before = jnp.cumsum(onehot, axis=1) - onehot
    slot_index = jnp.sum(before * onehot, axis=2)
    source = jnp.arange(N_OWN, dtype=jnp.int32)[:, None]
    target = (flat_ids * row_count + source * CAP + slot_index).astype(jnp.int32).reshape(TOKENS * TOP)
    in_buffer = jnp.zeros((EXPERTS * row_count, D), jnp.bfloat16).at[target].set(jnp.repeat(tokens, TOP, axis=0))
    weighted_cot = (route_weights[:, :, None] * cotangent.astype(jnp.float32)[:, None, :]).astype(jnp.bfloat16)
    cot_buffer = jnp.zeros((EXPERTS * row_count, D), jnp.bfloat16).at[target].set(weighted_cot.reshape(TOKENS * TOP, D))
    results = lax.map(expert_pass, (in_buffer.reshape(EXPERTS, row_count, D), cot_buffer.reshape(EXPERTS, row_count, D),
                                    to_experts(gate_weight), to_experts(up_weight), to_experts(down_weight_t)))
    outputs, row_grads, gate_grad, up_grad, down_grad = results
    picked = outputs.reshape(EXPERTS * row_count, D)[target].reshape(TOKENS, TOP, D)
    layer_out = jnp.sum(route_weights[:, :, None] * picked, axis=1).astype(jnp.bfloat16)
    picked_grad = row_grads.reshape(EXPERTS * row_count, D)[target].reshape(TOKENS, TOP, D)
    token_grad = jnp.sum(picked_grad, axis=1).astype(jnp.bfloat16)
    return layer_out, token_grad, to_tiles(gate_grad), to_tiles(up_grad), to_tiles(down_grad)
```

```python
import jax
import jax.numpy as jnp
from jax import lax
from jax.experimental import pallas as pl
from jax.experimental.pallas import tpu as pltpu
from jax.sharding import PartitionSpec as P

OWN = 32
SLOT = 16
TOK = 128
DQ = 512
FQ = 352
TOP = 6
ROWS = OWN * SLOT
BPC = 8
CHUNK = BPC * SLOT
HALF = FQ // 2
MESH = pl.DeviceIdType.MESH
F32 = jnp.float32
BF16 = jnp.bfloat16


def mm(lhs, rhs, contract=(1, 0)):
    return lax.dot_general(
        lhs,
        rhs,
        (((contract[0],), (contract[1],)), ((), ())),
        preferred_element_type=F32,
    )


def iota(shape, dim):
    return lax.broadcasted_iota(jnp.int32, shape, dim)


def kernel(
    ids_ref,
    wts_ref,
    tok_hbm,
    cot_hbm,
    gate_hbm,
    up_hbm,
    down_hbm,
    layer_ref,
    tgrad_ref,
    gate_out,
    up_out,
    down_out,
    tok,
    cot,
    wgt,
    sel_t,
    whi_t,
    wlo_t,
    send,
    recv,
    far,
    relay,
    near,
    landed,
    hid,
    back,
    home,
    part,
    cx_out,
    cx_in,
    pieces,
    bx_out,
    bx_in,
    grads,
    in_sem,
    d_send,
    d_recv,
    far_send,
    far_recv,
    rs_send,
    rs_recv,
    ag_send,
    ag_recv,
    r_send,
    r_recv,
    cx_sem,
    bx_send,
    bx_recv,
    out_sem,
):
    me = lax.axis_index("own")
    grp = lax.axis_index("grp")
    zl, xx, core = me // 8, me % 8 // 2, me % 2
    yy, bb = grp // 4, grp % 4
    aa, cc = yy // 2, yy % 2
    zz = bb * 4 + zl
    above, below, across = (aa + 1) % 4, (aa + 3) % 4, (aa + 2) % 4
    dev_above = (me, (above * 2 + cc) * 4 + bb)
    dev_below = (me, (below * 2 + cc) * 4 + bb)
    dev_pair = (me, (aa * 2 + 1 - cc) * 4 + bb)

    def dev_own(other):
        zl2, core2 = other // 8, other % 2
        gap = (zl2 - zl + 4) % 4
        two = 2 - 4 * ((zl // 2 + core + core2) % 2)
        hop = jnp.where(gap == 2, two, jnp.where(gap == 3, -1, gap))
        return (other, yy * 4 + (zz + hop + 16) % 16 // 4)

    def dev_b(k):
        return (me, yy * 4 + (bb + k) % 4)

    def remote(src, dst, ssem, rsem, dev):
        return pltpu.make_async_remote_copy(
            src_ref=src,
            dst_ref=dst,
            send_sem=ssem,
            recv_sem=rsem,
            device_id=dev,
            device_id_type=MESH,
        )

    cols = pl.ds(pl.multiple_of(aa * DQ, DQ), DQ)
    loads = [
        pltpu.make_async_copy(tok_hbm.at[:, cols], tok, in_sem.at[0]),
        pltpu.make_async_copy(cot_hbm.at[:, cols], cot, in_sem.at[1]),
        pltpu.make_async_copy(gate_hbm, wgt.at[0], in_sem.at[2]),
        pltpu.make_async_copy(up_hbm, wgt.at[1], in_sem.at[3]),
        pltpu.make_async_copy(down_hbm, wgt.at[2], in_sem.at[4]),
    ]
    for load in loads:
        load.start()

    barrier = pltpu.get_barrier_semaphore()

    def greet(dev):
        pl.semaphore_signal(barrier, inc=1, device_id=dev, device_id_type=MESH)

    @pl.loop(1, OWN)
    def _(step):
        greet(dev_own((me + step) % OWN))

    for dev in (dev_above, dev_below, dev_pair, dev_b(1), dev_b(2), dev_b(3)):
        greet(dev)

    expert = iota((OWN, TOK), 0) * 2 + cc
    named = jnp.zeros((OWN, TOK), F32)
    weight = jnp.zeros((OWN, TOK), F32)
    for k in range(TOP):
        hit = ids_ref[k : k + 1, :] == expert
        named = jnp.where(hit, 1.0, named)
        weight = jnp.where(hit, wts_ref[k : k + 1, :], weight)
    earlier = (iota((TOK, TOK), 0) < iota((TOK, TOK), 1)).astype(F32).astype(BF16)
    place = mm(named.astype(BF16), earlier)
    place = jnp.where(named > 0.5, place, -1.0).astype(BF16)
    spread = (iota((ROWS, OWN), 0) // SLOT == iota((ROWS, OWN), 1)).astype(F32).astype(BF16)
    place_rows = mm(spread, place)
    taken = place_rows == (iota((ROWS, TOK), 0) % SLOT).astype(F32)
    w1 = weight.astype(BF16)
    rest = weight - w1.astype(F32)
    w2 = rest.astype(BF16)
    w3 = (rest - w2.astype(F32)).astype(BF16)
    weight_rows = mm(spread, w1) + mm(spread, w2) + mm(spread, w3)
    sel = jnp.where(taken, 1.0, 0.0)
    wsel = jnp.where(taken, weight_rows, 0.0)
    row_weight = jnp.sum(wsel, axis=1, keepdims=True)
    sel16 = sel.astype(BF16)

    loads[0].wait()
    send[0] = mm(sel16, tok[...]).astype(BF16).reshape(OWN, SLOT, DQ)
    loads[1].wait()
    send[1] = (row_weight * mm(sel16, cot[...])).astype(BF16).reshape(OWN, SLOT, DQ)

    pl.semaphore_wait(barrier, OWN - 1 + 6)

    for chunk in (across, above, below, aa):

        @pl.loop(0, BPC)
        def _(step, chunk=chunk):
            dl, core2 = step // 2, step % 2
            other = (zl - dl + 4) % 4 * 8 + (xx + dl - chunk + 8) % 4 * 2 + core2
            pos = chunk * BPC + dl * 2 + core

            @pl.when(other == me)
            def _():
                pltpu.make_async_copy(send.at[:, other], recv.at[:, pos], d_recv.at[chunk]).start()

            @pl.when(other != me)
            def _():
                remote(
                    send.at[:, other], recv.at[:, pos], d_send, d_recv.at[chunk], dev_own(other)
                ).start()

    wsel_t = wsel.T
    hi = wsel_t.astype(BF16)
    whi_t[...] = hi
    wlo_t[...] = (wsel_t - hi.astype(F32)).astype(BF16)
    sel_t[...] = sel.T.astype(BF16)
    for load in loads[2:]:
        load.wait()

    lower, upper = pl.ds(0, HALF), pl.ds(HALF, HALF)

    def rows_of(chunk):
        return pl.ds(chunk * BPC, BPC)

    def lanes_of(chunk):
        return pl.ds(pl.multiple_of(chunk * CHUNK, CHUNK), CHUNK)

    def partials(chunk):
        block = recv.at[:, rows_of(chunk)]
        pltpu.make_async_copy(block, block, d_recv.at[chunk]).wait()
        x_rows = recv[0, rows_of(chunk)].reshape(CHUNK, DQ)
        c_rows = recv[1, rows_of(chunk)].reshape(CHUNK, DQ)
        return [mm(wgt[t], rows, (1, 1)) for t, rows in enumerate((x_rows, x_rows, c_rows))]

    for t, value in enumerate(partials(across)):
        far[t] = value.astype(BF16)
    far_copies = [
        remote(far.at[:, lower], relay.at[0], far_send.at[0], far_recv.at[0], dev_above),
        remote(far.at[:, upper], relay.at[1], far_send.at[1], far_recv.at[1], dev_below),
    ]
    for copy in far_copies:
        copy.start()
    rs_copies = []
    for way, chunk, dev in ((0, above, dev_above), (1, below, dev_below)):
        values = partials(chunk)
        far_copies[way].wait_recv()
        for t, value in enumerate(values):
            first, second = value[:HALF], value[HALF:]
            if way == 0:
                first = first + relay[0, t].astype(F32)
            else:
                second = second + relay[1, t].astype(F32)
            near[way, t, :HALF] = first.astype(BF16)
            near[way, t, HALF:] = second.astype(BF16)
        copy = remote(near.at[way], landed.at[way], rs_send.at[way], rs_recv.at[way], dev)
        copy.start()
        rs_copies.append(copy)
    mine = partials(aa)
    for copy in rs_copies:
        copy.wait_recv()
    gating, up_proj, grad_hidden = [
        value + landed[0, t].astype(F32) + landed[1, t].astype(F32) for t, value in enumerate(mine)
    ]
    sigma = jax.nn.sigmoid(gating)
    grad_gate = grad_hidden * up_proj * sigma * (1.0 + gating * (1.0 - sigma))
    hid[0, :, lanes_of(aa)] = (gating * sigma * up_proj).astype(BF16)
    hid[1, :, lanes_of(aa)] = grad_gate.astype(BF16)
    hid[2, :, lanes_of(aa)] = (grad_hidden * gating * sigma).astype(BF16)

    def pass_on(index, chunk, half, dev):
        block = hid.at[:, half, lanes_of(chunk)]
        return remote(block, block, ag_send.at[index], ag_recv.at[index], dev)

    up_a = pass_on(0, aa, lower, dev_above)
    down_b = pass_on(1, aa, upper, dev_below)
    up_b = pass_on(2, aa, upper, dev_above)
    down_a = pass_on(3, aa, lower, dev_below)
    for copy in (up_a, down_b, up_b, down_a):
        copy.start()

    def arrived(index, chunk, half):
        block = hid.at[:, half, lanes_of(chunk)]
        pltpu.make_async_copy(block, block, ag_recv.at[index]).wait()

    def give_back(chunk):
        lanes = lanes_of(chunk)
        out_rows = mm(hid[0, :, lanes], wgt[2], (0, 0))
        grad_rows = mm(hid[1, :, lanes], wgt[0], (0, 0)) + mm(hid[2, :, lanes], wgt[1], (0, 0))
        back[0, rows_of(chunk)] = out_rows.astype(BF16).reshape(BPC, SLOT, DQ)
        back[1, rows_of(chunk)] = grad_rows.astype(BF16).reshape(BPC, SLOT, DQ)

        @pl.loop(0, BPC)
        def _(step):
            dl, core2 = step // 2, step % 2
            other = (zl + dl) % 4 * 8 + (xx + chunk - dl + 4) % 4 * 2 + core2
            pos = chunk * BPC + step

            @pl.when(other == me)
            def _():
                pltpu.make_async_copy(back.at[:, pos], home.at[:, me], r_recv).start()

            @pl.when(other != me)
            def _():
                remote(back.at[:, pos], home.at[:, me], r_send, r_recv, dev_own(other)).start()

    give_back(aa)
    arrived(0, below, lower)
    on_up = pass_on(4, below, lower, dev_above)
    on_up.start()
    arrived(1, above, upper)
    on_down = pass_on(5, above, upper, dev_below)
    on_down.start()
    arrived(2, below, upper)
    give_back(below)
    arrived(3, above, lower)
    give_back(above)
    arrived(4, across, lower)
    arrived(5, across, upper)
    give_back(across)

    stores = []
    for t, (side, kind, out) in enumerate(((0, 1, gate_out), (0, 2, up_out), (1, 0, down_out))):
        grads[t] = mm(hid[kind], recv[side].reshape(ROWS, DQ))
        store = pltpu.make_async_copy(grads.at[t], out, out_sem.at[t])
        store.start()
        stores.append(store)

    pltpu.make_async_copy(home, home, r_recv).wait()
    out_home = home[0].reshape(ROWS, DQ)
    part[0] = mm(whi_t[...], out_home) + mm(wlo_t[...], out_home)
    part[1] = mm(sel_t[...], home[1].reshape(ROWS, DQ))

    kept = pl.ds(pl.multiple_of(cc * 256, 256), 256)
    given = pl.ds(pl.multiple_of((1 - cc) * 256, 256), 256)
    cx_out[...] = part[:, :, given].astype(BF16)
    cx = remote(cx_out, cx_in, cx_sem.at[0], cx_sem.at[1], dev_pair)
    cx.start()
    cx.wait_recv()
    total = part[:, :, kept] + cx_in[...].astype(F32)
    for p in range(4):
        piece = jnp.concatenate(
            [total[0, :, 64 * p : 64 * p + 64], total[1, :, 64 * p : 64 * p + 64]], axis=1
        )
        pieces[p] = piece
        bx_out[p] = piece.astype(BF16)
    bx = []
    for k in (1, 2, 3):
        copy = remote(
            bx_out.at[(bb + k) % 4],
            bx_in.at[k - 1],
            bx_send.at[k - 1],
            bx_recv.at[k - 1],
            dev_b(k),
        )
        copy.start()
        bx.append(copy)
    final = pieces[bb]
    for k in range(3):
        bx[k].wait_recv()
        final = final + bx_in[k].astype(F32)
    layer_ref[...] = final[:, :64].astype(BF16)
    tgrad_ref[...] = final[:, 64:].astype(BF16)

    pltpu.make_async_copy(send.at[:, : OWN - 1], recv.at[:, : OWN - 1], d_send).wait()
    pltpu.make_async_copy(back.at[:, : OWN - 1], home.at[:, : OWN - 1], r_send).wait()
    for copy in far_copies + rs_copies + [up_a, down_b, up_b, down_a, on_up, on_down, cx] + bx:
        copy.wait_send()
    for store in stores:
        store.wait()


def on_device(tokens, cotangent, route_ids, route_weights, gate_weight, up_weight, down_weight_t):
    vmem = pl.BlockSpec(memory_space=pltpu.VMEM)
    hbm = pl.BlockSpec(memory_space=pl.ANY)
    dma = pltpu.SemaphoreType.DMA
    grad_shape = jax.ShapeDtypeStruct((FQ, DQ), F32)
    out_shape = jax.ShapeDtypeStruct((TOK, 64), BF16)
    layer_out, token_grad, gate_grad, up_grad, down_grad = pl.pallas_call(
        kernel,
        out_shape=(out_shape, out_shape, grad_shape, grad_shape, grad_shape),
        in_specs=[vmem, vmem, hbm, hbm, hbm, hbm, hbm],
        out_specs=(vmem, vmem, hbm, hbm, hbm),
        scratch_shapes=[
            pltpu.VMEM((TOK, DQ), BF16),
            pltpu.VMEM((TOK, DQ), BF16),
            pltpu.VMEM((3, FQ, DQ), BF16),
            pltpu.VMEM((TOK, ROWS), BF16),
            pltpu.VMEM((TOK, ROWS), BF16),
            pltpu.VMEM((TOK, ROWS), BF16),
            pltpu.VMEM((2, OWN, SLOT, DQ), BF16),
            pltpu.VMEM((2, OWN, SLOT, DQ), BF16),
            pltpu.VMEM((3, FQ, CHUNK), BF16),
            pltpu.VMEM((2, 3, HALF, CHUNK), BF16),
            pltpu.VMEM((2, 3, FQ, CHUNK), BF16),
            pltpu.VMEM((2, 3, FQ, CHUNK), BF16),
            pltpu.VMEM((3, FQ, ROWS), BF16),
            pltpu.VMEM((2, OWN, SLOT, DQ), BF16),
            pltpu.VMEM((2, OWN, SLOT, DQ), BF16),
            pltpu.VMEM((2, TOK, DQ), F32),
            pltpu.VMEM((2, TOK, 256), BF16),
            pltpu.VMEM((2, TOK, 256), BF16),
            pltpu.VMEM((4, TOK, 128), F32),
            pltpu.VMEM((4, TOK, 128), BF16),
            pltpu.VMEM((3, TOK, 128), BF16),
            pltpu.VMEM((3, FQ, DQ), F32),
            dma((5,)),
            dma,
            dma((4,)),
            dma((2,)),
            dma((2,)),
            dma((2,)),
            dma((2,)),
            dma((6,)),
            dma((6,)),
            dma,
            dma,
            dma((2,)),
            dma((3,)),
            dma((3,)),
            dma((3,)),
        ],
        compiler_params=pltpu.CompilerParams(
            collective_id=0, has_side_effects=True, vmem_limit_bytes=40 * 1024 * 1024
        ),
        cost_estimate=pl.CostEstimate(
            flops=2 * 9 * ROWS * DQ * FQ, bytes_accessed=8 * 1024 * 1024, transcendentals=CHUNK * FQ
        ),
    )(
        route_ids.T,
        route_weights.T,
        tokens,
        cotangent,
        gate_weight[0].T,
        up_weight[0].T,
        down_weight_t[0].T,
    )
    return (layer_out, token_grad, gate_grad.T[None], up_grad.T[None], down_grad.T[None])


def solution(mesh):
    placed = (
        P("own", None),
        P("own", None),
        P("own", None),
        P("own", None),
        P(("own", "grp"), None, None),
        P(("own", "grp"), None, None),
        P(("own", "grp"), None, None),
    )
    return jax.shard_map(
        on_device,
        mesh=mesh,
        in_specs=placed,
        out_specs=(
            P("own", "grp"),
            P("own", "grp"),
            P(("own", "grp"), None, None),
            P(("own", "grp"), None, None),
            P(("own", "grp"), None, None),
        ),
        check_vma=False,
    )
```

```python
import jax
import jax.numpy as jnp
from jax import lax
from jax.experimental import pallas as pl
from jax.experimental.pallas import tpu as pltpu
from jax.sharding import PartitionSpec as P

OWN = 32
SLOT = 16
TOK = 128
DQ = 512
FQ = 352
TOP = 6
ROWS = OWN * SLOT
BPC = 8
CHUNK = BPC * SLOT
QUARTERS = ((0, 96), (96, 80), (176, 96), (272, 80))
UP, DOWN = 0, 1
RELAYED = ((0, 1), (2, 3))
VMEM_LIMIT = 58 * 1024 * 1024
MESH = pl.DeviceIdType.MESH
F32 = jnp.float32
BF16 = jnp.bfloat16


def mm(lhs, rhs, contract=(1, 0)):
    return lax.dot_general(
        lhs,
        rhs,
        (((contract[0],), (contract[1],)), ((), ())),
        preferred_element_type=F32,
    )


def iota(shape, dim):
    return lax.broadcasted_iota(jnp.int32, shape, dim)


def kernel(
    ids_hbm,
    wts_hbm,
    tok_hbm,
    cot_hbm,
    gate_hbm,
    up_hbm,
    down_hbm,
    layer_ref,
    tgrad_ref,
    gate_out,
    up_out,
    down_out,
    ids_ref,
    wts_ref,
    tok,
    cot,
    wgt,
    sel16,
    row_w,
    sel_t,
    whi_t,
    wlo_t,
    send,
    recv,
    far,
    relay,
    near,
    keep,
    mine,
    landed,
    hid,
    back,
    home,
    part,
    cx_out,
    cx_in,
    pieces,
    bx_out,
    bx_in,
    in_sem,
    d_send,
    d_recv,
    far_send,
    far_recv,
    rs_send,
    rs_recv,
    ag_send,
    ag_recv,
    fw_send,
    fw_recv,
    r_send,
    r_recv,
    cx_sem,
    bx_send,
    bx_recv,
):
    me = lax.axis_index("own")
    grp = lax.axis_index("grp")
    zl, xx, core = me // 8, me % 8 // 2, me % 2
    yy, bb = grp // 4, grp % 4
    aa, cc = yy // 2, yy % 2
    zz = bb * 4 + zl
    above, below, across = (aa + 1) % 4, (aa + 3) % 4, (aa + 2) % 4
    dev_above = (me, (above * 2 + cc) * 4 + bb)
    dev_below = (me, (below * 2 + cc) * 4 + bb)
    dev_pair = (me, (aa * 2 + 1 - cc) * 4 + bb)

    def dev_own(other):
        zl2, core2 = other // 8, other % 2
        gap = (zl2 - zl + 4) % 4
        two = 2 - 4 * ((zl // 2 + core + core2) % 2)
        hop = jnp.where(gap == 2, two, jnp.where(gap == 3, -1, gap))
        return (other, yy * 4 + (zz + hop + 16) % 16 // 4)

    def dev_b(k):
        return (me, yy * 4 + (bb + k) % 4)

    def remote(src, dst, ssem, rsem, dev):
        return pltpu.make_async_remote_copy(
            src_ref=src,
            dst_ref=dst,
            send_sem=ssem,
            recv_sem=rsem,
            device_id=dev,
            device_id_type=MESH,
        )

    cols = pl.ds(pl.multiple_of(aa * DQ, DQ), DQ)
    loads = [
        pltpu.make_async_copy(ids_hbm, ids_ref, in_sem.at[5]),
        pltpu.make_async_copy(wts_hbm, wts_ref, in_sem.at[6]),
        pltpu.make_async_copy(tok_hbm.at[:, cols], tok, in_sem.at[0]),
        pltpu.make_async_copy(cot_hbm.at[:, cols], cot, in_sem.at[1]),
        pltpu.make_async_copy(gate_hbm, wgt.at[0], in_sem.at[2]),
        pltpu.make_async_copy(up_hbm, wgt.at[1], in_sem.at[3]),
        pltpu.make_async_copy(down_hbm, wgt.at[2], in_sem.at[4]),
    ]
    for load in loads:
        load.start()

    barrier = pltpu.get_barrier_semaphore()

    def greet(dev):
        pl.semaphore_signal(barrier, inc=1, device_id=dev, device_id_type=MESH)

    @pl.loop(1, OWN)
    def _(step):
        greet(dev_own((me + step) % OWN))

    for dev in (dev_above, dev_below, dev_pair, dev_b(1), dev_b(2), dev_b(3)):
        greet(dev)

    loads[0].wait()
    loads[1].wait()
    expert = iota((OWN, TOK), 0) * 2 + cc
    named = jnp.zeros((OWN, TOK), F32)
    weight = jnp.zeros((OWN, TOK), F32)
    for k in range(TOP):
        hit = ids_ref[k : k + 1, :] == expert
        named = jnp.where(hit, 1.0, named)
        weight = jnp.where(hit, wts_ref[k : k + 1, :], weight)
    earlier = (iota((TOK, TOK), 0) < iota((TOK, TOK), 1)).astype(F32).astype(BF16)
    place = mm(named.astype(BF16), earlier)
    place = jnp.where(named > 0.5, place, -1.0).astype(BF16)
    pos_of = iota((ROWS, OWN), 0) // SLOT
    step_of = pos_of % BPC // 2
    owner_of = (zl - step_of + 4) % 4 * 8 + (xx + step_of - pos_of // BPC + 8) % 4 * 2 + pos_of % 2
    spread = (owner_of == iota((ROWS, OWN), 1)).astype(F32).astype(BF16)
    place_rows = mm(spread, place)
    taken = place_rows == (iota((ROWS, TOK), 0) % SLOT).astype(F32)
    w1 = weight.astype(BF16)
    rest = weight - w1.astype(F32)
    w2 = rest.astype(BF16)
    w3 = (rest - w2.astype(F32)).astype(BF16)
    weight_rows = mm(spread, w1) + mm(spread, w2) + mm(spread, w3)
    sel = jnp.where(taken, 1.0, 0.0)
    wsel = jnp.where(taken, weight_rows, 0.0)
    row_weight = jnp.sum(wsel, axis=1, keepdims=True)
    sel16[...] = sel.astype(BF16)
    row_w[...] = row_weight

    for load in loads[2:4]:
        load.wait()

    def rows_of(chunk):
        return pl.ds(chunk * BPC, BPC)

    def lanes_of(chunk):
        return pl.ds(pl.multiple_of(chunk * CHUNK, CHUNK), CHUNK)

    for order, chunk in enumerate((across, above, below, aa)):
        picks = sel16[lanes_of(chunk), :]
        x_rows = mm(picks, tok[...])
        c_rows = row_w[lanes_of(chunk), :] * mm(picks, cot[...])
        send[0, rows_of(chunk)] = x_rows.astype(BF16).reshape(BPC, SLOT, DQ)
        send[1, rows_of(chunk)] = c_rows.astype(BF16).reshape(BPC, SLOT, DQ)
        if order == 0:
            pl.semaphore_wait(barrier, OWN - 1 + 6)

        @pl.loop(0, BPC)
        def _(step, chunk=chunk):
            dl, core2 = step // 2, step % 2
            other = (zl - dl + 4) % 4 * 8 + (xx + dl - chunk + 8) % 4 * 2 + core2
            src = send.at[:, chunk * BPC + step]
            dst = recv.at[:, chunk * BPC + dl * 2 + core]

            @pl.when(other == me)
            def _():
                pltpu.make_async_copy(src, dst, d_recv.at[chunk]).start()

            @pl.when(other != me)
            def _():
                remote(src, dst, d_send, d_recv.at[chunk], dev_own(other)).start()

    wsel_t = wsel.T
    hi = wsel_t.astype(BF16)
    whi_t[...] = hi
    wlo_t[...] = (wsel_t - hi.astype(F32)).astype(BF16)
    sel_t[...] = sel.T.astype(BF16)
    for load in loads[4:]:
        load.wait()

    def partials(chunk):
        block = recv.at[:, rows_of(chunk)]
        pltpu.make_async_copy(block, block, d_recv.at[chunk]).wait()
        x_rows = recv[0, rows_of(chunk)].reshape(CHUNK, DQ)
        c_rows = recv[1, rows_of(chunk)].reshape(CHUNK, DQ)
        return [mm(wgt[t], rows, (1, 1)) for t, rows in enumerate((x_rows, x_rows, c_rows))]

    def units(quarter):
        return pl.ds(*QUARTERS[quarter])

    devs = (dev_above, dev_below)
    copies = {}

    def go(kind, way, quarter, src, dst, sems):
        index = 4 * way + quarter
        copy = remote(src, dst, sems[0].at[index], sems[1].at[index], devs[way])
        copy.start()
        copies[kind, way, quarter] = copy

    def send_near(way, quarter):
        block = (way, slice(None), units(quarter))
        go("near", way, quarter, near.at[block], landed.at[block], (rs_send, rs_recv))

    for t, value in enumerate(partials(across)):
        far[t] = value.astype(BF16)
    for i in range(2):
        for way in (UP, DOWN):
            quarter = RELAYED[way][i]
            block = (slice(None), units(quarter))
            go("far", way, quarter, far.at[block], relay.at[block], (far_send, far_recv))
    for way, chunk in ((UP, above), (DOWN, below)):
        for t, value in enumerate(partials(chunk)):
            keep[way, t] = value
            near[way, t] = value.astype(BF16)
        send_near(way, RELAYED[1 - way][0])
    for i in range(2):
        for way in (UP, DOWN):
            quarter = RELAYED[way][i]
            copies["far", way, quarter].wait_recv()
            summed = keep[way, :, units(quarter)] + relay[:, units(quarter)].astype(F32)
            near[way, :, units(quarter)] = summed.astype(BF16)
            send_near(way, quarter)
        if i == 0:
            for way in (UP, DOWN):
                send_near(way, RELAYED[1 - way][1])
            for t, value in enumerate(partials(aa)):
                mine[t] = value

    def pass_on(kind, way, chunk, quarter, sems):
        block = hid.at[:, units(quarter), lanes_of(chunk)]
        go(kind, way, quarter, block, block, sems)

    def arrived(sems, way, chunk, quarter):
        block = hid.at[:, units(quarter), lanes_of(chunk)]
        pltpu.make_async_copy(block, block, sems.at[4 * way + quarter]).wait()

    for quarter in (0, 2, 1, 3):
        copies["near", UP, quarter].wait_recv()
        copies["near", DOWN, quarter].wait_recv()
        span = units(quarter)
        gating, up_proj, grad_hidden = [
            mine[t, span] + landed[UP, t, span].astype(F32) + landed[DOWN, t, span].astype(F32)
            for t in range(3)
        ]
        sigma = jax.nn.sigmoid(gating)
        grad_gate = grad_hidden * up_proj * sigma * (1.0 + gating * (1.0 - sigma))
        hid[0, span, lanes_of(aa)] = (gating * sigma * up_proj).astype(BF16)
        hid[1, span, lanes_of(aa)] = grad_gate.astype(BF16)
        hid[2, span, lanes_of(aa)] = (grad_hidden * gating * sigma).astype(BF16)
        first = UP if quarter in RELAYED[UP] else DOWN
        for way in (first, 1 - first):
            pass_on("own", way, aa, quarter, (ag_send, ag_recv))

    def give_back(chunk):
        lanes = lanes_of(chunk)
        out_rows = mm(hid[0, :, lanes], wgt[2], (0, 0))
        grad_rows = mm(hid[1, :, lanes], wgt[0], (0, 0)) + mm(hid[2, :, lanes], wgt[1], (0, 0))
        back[0, rows_of(chunk)] = out_rows.astype(BF16).reshape(BPC, SLOT, DQ)
        back[1, rows_of(chunk)] = grad_rows.astype(BF16).reshape(BPC, SLOT, DQ)

        @pl.loop(0, BPC)
        def _(step):
            dl, core2 = step // 2, step % 2
            other = (zl + dl) % 4 * 8 + (xx + chunk - dl + 4) % 4 * 2 + core2
            src = back.at[:, chunk * BPC + step]
            dst = home.at[:, chunk * BPC + dl * 2 + core]

            @pl.when(other == me)
            def _():
                pltpu.make_async_copy(src, dst, r_recv.at[chunk]).start()

            @pl.when(other != me)
            def _():
                remote(src, dst, r_send, r_recv.at[chunk], dev_own(other)).start()

    for i in range(2):
        for way, chunk in ((UP, below), (DOWN, above)):
            quarter = RELAYED[way][i]
            arrived(ag_recv, way, chunk, quarter)
            pass_on("on", way, chunk, quarter, (fw_send, fw_recv))
        if i == 0:
            give_back(aa)
    for way, chunk in ((UP, below), (DOWN, above)):
        for quarter in RELAYED[1 - way]:
            arrived(ag_recv, way, chunk, quarter)
        give_back(chunk)
    for way in (UP, DOWN):
        for quarter in RELAYED[way]:
            arrived(fw_recv, way, across, quarter)
    give_back(across)

    def combine(chunk):
        block = home.at[:, rows_of(chunk)]
        pltpu.make_async_copy(block, block, r_recv.at[chunk]).wait()
        lanes = lanes_of(chunk)
        out_home = home[0, rows_of(chunk)].reshape(CHUNK, DQ)
        grad_home = home[1, rows_of(chunk)].reshape(CHUNK, DQ)
        return (
            mm(whi_t[:, lanes], out_home) + mm(wlo_t[:, lanes], out_home),
            mm(sel_t[:, lanes], grad_home),
        )

    part[0], part[1] = combine(aa)
    for chunk in (below, above):
        layer, tgrad = combine(chunk)
        part[0] += layer
        part[1] += tgrad

    for side, kind, out in ((0, 1, gate_out), (0, 2, up_out), (1, 0, down_out)):
        out[...] = mm(hid[kind], recv[side].reshape(ROWS, DQ))

    layer, tgrad = combine(across)
    part[0] += layer
    part[1] += tgrad

    kept = pl.ds(pl.multiple_of(cc * 256, 256), 256)
    given = pl.ds(pl.multiple_of((1 - cc) * 256, 256), 256)
    cx_out[...] = part[:, :, given].astype(BF16)
    cx = remote(cx_out, cx_in, cx_sem.at[0], cx_sem.at[1], dev_pair)
    cx.start()
    cx.wait_recv()
    total = part[:, :, kept] + cx_in[...].astype(F32)
    for p in range(4):
        piece = jnp.concatenate(
            [total[0, :, 64 * p : 64 * p + 64], total[1, :, 64 * p : 64 * p + 64]], axis=1
        )
        pieces[p] = piece
        bx_out[p] = piece.astype(BF16)
    bx = []
    for k in (1, 2, 3):
        copy = remote(
            bx_out.at[(bb + k) % 4],
            bx_in.at[k - 1],
            bx_send.at[k - 1],
            bx_recv.at[k - 1],
            dev_b(k),
        )
        copy.start()
        bx.append(copy)
    final = pieces[bb]
    for k in range(3):
        bx[k].wait_recv()
        final = final + bx_in[k].astype(F32)
    final = final.T
    layer_ref[...] = final[:64].astype(BF16)
    tgrad_ref[...] = final[64:].astype(BF16)

    pltpu.make_async_copy(send.at[:, : OWN - 1], recv.at[:, : OWN - 1], d_send).wait()
    pltpu.make_async_copy(back.at[:, : OWN - 1], home.at[:, : OWN - 1], r_send).wait()
    for copy in list(copies.values()) + [cx] + bx:
        copy.wait_send()


def finish(*refs):
    given, out, held = refs[:5], refs[5:10], refs[10:15]
    in_sem, out_sem = refs[15:]
    loads = [pltpu.make_async_copy(given[i], held[i], in_sem.at[i]) for i in range(5)]
    stores = [pltpu.make_async_copy(held[i], out[i], out_sem.at[i]) for i in range(5)]
    for load in loads:
        load.start()
    for load, store in zip(loads, stores):
        load.wait()
        store.start()
    for store in stores:
        store.wait()


def on_device(tokens, cotangent, route_ids, route_weights, gate_weight, up_weight, down_weight_t):
    vmem = pl.BlockSpec(memory_space=pltpu.VMEM)
    hbm = pl.BlockSpec(memory_space=pl.ANY)
    dma = pltpu.SemaphoreType.DMA
    grad_shape = jax.ShapeDtypeStruct((FQ, DQ), F32)
    out_shape = jax.ShapeDtypeStruct((64, TOK), BF16)
    out_shapes = (out_shape, out_shape, grad_shape, grad_shape, grad_shape)
    results = pl.pallas_call(
        kernel,
        out_shape=out_shapes,
        in_specs=[hbm] * 7,
        out_specs=(vmem,) * 5,
        scratch_shapes=[
            pltpu.VMEM((TOP, TOK), jnp.int32),
            pltpu.VMEM((TOP, TOK), F32),
            pltpu.VMEM((TOK, DQ), BF16),
            pltpu.VMEM((TOK, DQ), BF16),
            pltpu.VMEM((3, FQ, DQ), BF16),
            pltpu.VMEM((ROWS, TOK), BF16),
            pltpu.VMEM((ROWS, 1), F32),
            pltpu.VMEM((TOK, ROWS), BF16),
            pltpu.VMEM((TOK, ROWS), BF16),
            pltpu.VMEM((TOK, ROWS), BF16),
            pltpu.VMEM((2, OWN, SLOT, DQ), BF16),
            pltpu.VMEM((2, OWN, SLOT, DQ), BF16),
            pltpu.VMEM((3, FQ, CHUNK), BF16),
            pltpu.VMEM((3, FQ, CHUNK), BF16),
            pltpu.VMEM((2, 3, FQ, CHUNK), BF16),
            pltpu.VMEM((2, 3, FQ, CHUNK), F32),
            pltpu.VMEM((3, FQ, CHUNK), F32),
            pltpu.VMEM((2, 3, FQ, CHUNK), BF16),
            pltpu.VMEM((3, FQ, ROWS), BF16),
            pltpu.VMEM((2, OWN, SLOT, DQ), BF16),
            pltpu.VMEM((2, OWN, SLOT, DQ), BF16),
            pltpu.VMEM((2, TOK, DQ), F32),
            pltpu.VMEM((2, TOK, 256), BF16),
            pltpu.VMEM((2, TOK, 256), BF16),
            pltpu.VMEM((4, TOK, 128), F32),
            pltpu.VMEM((4, TOK, 128), BF16),
            pltpu.VMEM((3, TOK, 128), BF16),
            dma((7,)),
            dma,
            dma((4,)),
            dma((8,)),
            dma((8,)),
            dma((8,)),
            dma((8,)),
            dma((8,)),
            dma((8,)),
            dma((8,)),
            dma((8,)),
            dma,
            dma((4,)),
            dma((2,)),
            dma((3,)),
            dma((3,)),
        ],
        compiler_params=pltpu.CompilerParams(
            collective_id=0, has_side_effects=True, vmem_limit_bytes=VMEM_LIMIT
        ),
        cost_estimate=pl.CostEstimate(
            flops=2 * 9 * ROWS * DQ * FQ, bytes_accessed=8 * 1024 * 1024, transcendentals=CHUNK * FQ
        ),
    )(
        route_ids.T,
        route_weights.T,
        tokens,
        cotangent,
        gate_weight[0].T,
        up_weight[0].T,
        down_weight_t[0].T,
    )
    layer_out, token_grad, gate_grad, up_grad, down_grad = pl.pallas_call(
        finish,
        out_shape=out_shapes,
        in_specs=[hbm] * 5,
        out_specs=(hbm,) * 5,
        scratch_shapes=[pltpu.VMEM(s.shape, s.dtype) for s in out_shapes] + [dma((5,)), dma((5,))],
        compiler_params=pltpu.CompilerParams(vmem_limit_bytes=VMEM_LIMIT),
        cost_estimate=pl.CostEstimate(
            flops=0, bytes_accessed=6 * DQ * FQ * 4, transcendentals=0
        ),
    )(*results)
    return (layer_out.T, token_grad.T, gate_grad.T[None], up_grad.T[None], down_grad.T[None])


def solution(mesh):
    placed = (
        P("own", None),
        P("own", None),
        P("own", None),
        P("own", None),
        P(("own", "grp"), None, None),
        P(("own", "grp"), None, None),
        P(("own", "grp"), None, None),
    )
    return jax.shard_map(
        on_device,
        mesh=mesh,
        in_specs=placed,
        out_specs=(
            P("own", "grp"),
            P("own", "grp"),
            P(("own", "grp"), None, None),
            P(("own", "grp"), None, None),
            P(("own", "grp"), None, None),
        ),
        check_vma=False,
    )
```

```python
import jax
import jax.numpy as jnp
from jax import lax
from jax.experimental import pallas as pl
from jax.experimental.pallas import tpu as pltpu
from jax.sharding import PartitionSpec as P

OWN = 32
SLOT = 16
TOK = 128
DQ = 512
FQ = 352
TOP = 6
ROWS = OWN * SLOT
BPC = 8
CHUNK = BPC * SLOT
QUARTERS = ((0, 96), (96, 80), (176, 96), (272, 80))
UP, DOWN = 0, 1
RELAYED = ((0, 1), (2, 3))
VMEM_LIMIT = 58 * 1024 * 1024
MESH = pl.DeviceIdType.MESH
F32 = jnp.float32
BF16 = jnp.bfloat16


def mm(lhs, rhs, contract=(1, 0)):
    return lax.dot_general(
        lhs,
        rhs,
        (((contract[0],), (contract[1],)), ((), ())),
        preferred_element_type=F32,
    )


def iota(shape, dim):
    return lax.broadcasted_iota(jnp.int32, shape, dim)


def kernel(
    ids_hbm,
    wts_hbm,
    tok_hbm,
    cot_hbm,
    gate_hbm,
    up_hbm,
    down_hbm,
    layer_ref,
    tgrad_ref,
    gate_out,
    up_out,
    down_out,
    ids_ref,
    wts_ref,
    tok,
    cot,
    wgt,
    sel16,
    wsel_ref,
    sel_t,
    whi_t,
    wlo_t,
    send,
    recv,
    far,
    relay,
    near,
    keep,
    mine,
    landed,
    hid,
    back,
    home,
    part,
    cx_out,
    cx_in,
    pieces,
    bx_out,
    bx_in,
    in_sem,
    d_send,
    d_recv,
    far_send,
    far_recv,
    rs_send,
    rs_recv,
    ag_send,
    ag_recv,
    fw_send,
    fw_recv,
    r_send,
    r_recv,
    cx_send,
    cx_recv,
    bx_send,
    bx_recv,
):
    me = lax.axis_index("own")
    grp = lax.axis_index("grp")
    zl, xx, core = me // 8, me % 8 // 2, me % 2
    yy, bb = grp // 4, grp % 4
    aa, cc = yy // 2, yy % 2
    zz = bb * 4 + zl
    above, below, across = (aa + 1) % 4, (aa + 3) % 4, (aa + 2) % 4
    dev_above = (me, (above * 2 + cc) * 4 + bb)
    dev_below = (me, (below * 2 + cc) * 4 + bb)
    dev_pair = (me, (aa * 2 + 1 - cc) * 4 + bb)

    def dev_own(other):
        zl2, core2 = other // 8, other % 2
        gap = (zl2 - zl + 4) % 4
        two = 2 - 4 * ((zl // 2 + core + core2) % 2)
        hop = jnp.where(gap == 2, two, jnp.where(gap == 3, -1, gap))
        return (other, yy * 4 + (zz + hop + 16) % 16 // 4)

    def dev_b(k):
        return (me, yy * 4 + (bb + k) % 4)

    def remote(src, dst, ssem, rsem, dev):
        return pltpu.make_async_remote_copy(
            src_ref=src,
            dst_ref=dst,
            send_sem=ssem,
            recv_sem=rsem,
            device_id=dev,
            device_id_type=MESH,
        )

    cols = pl.ds(pl.multiple_of(aa * DQ, DQ), DQ)
    loads = [
        pltpu.make_async_copy(ids_hbm, ids_ref, in_sem.at[5]),
        pltpu.make_async_copy(wts_hbm, wts_ref, in_sem.at[6]),
        pltpu.make_async_copy(tok_hbm.at[:, cols], tok, in_sem.at[0]),
        pltpu.make_async_copy(cot_hbm.at[:, cols], cot, in_sem.at[1]),
        pltpu.make_async_copy(gate_hbm, wgt.at[0], in_sem.at[2]),
        pltpu.make_async_copy(up_hbm, wgt.at[1], in_sem.at[3]),
        pltpu.make_async_copy(down_hbm, wgt.at[2], in_sem.at[4]),
    ]
    for load in loads:
        load.start()

    barrier = pltpu.get_barrier_semaphore()

    def greet(dev):
        pl.semaphore_signal(barrier, inc=1, device_id=dev, device_id_type=MESH)

    @pl.loop(1, OWN)
    def _(step):
        greet(dev_own((me + step) % OWN))

    for dev in (dev_above, dev_below, dev_pair, dev_b(1), dev_b(3)):
        greet(dev)

    loads[0].wait()
    loads[1].wait()
    expert = iota((OWN, TOK), 0) * 2 + cc
    named = jnp.zeros((OWN, TOK), F32)
    weight = jnp.zeros((OWN, TOK), F32)
    for k in range(TOP):
        hit = ids_ref[k : k + 1, :] == expert
        named = jnp.where(hit, 1.0, named)
        weight = jnp.where(hit, wts_ref[k : k + 1, :], weight)
    earlier = (iota((TOK, TOK), 0) < iota((TOK, TOK), 1)).astype(F32).astype(BF16)
    place = mm(named.astype(BF16), earlier)
    place = jnp.where(named > 0.5, place, -1.0).astype(BF16)
    w1 = weight.astype(BF16)
    rest = weight - w1.astype(F32)
    w2 = rest.astype(BF16)
    w3 = (rest - w2.astype(F32)).astype(BF16)
    for load in loads[2:4]:
        load.wait()

    def rows_of(chunk):
        return pl.ds(chunk * BPC, BPC)

    def lanes_of(chunk):
        return pl.ds(pl.multiple_of(chunk * CHUNK, CHUNK), CHUNK)

    def dispatch(chunk, first=False):
        pos_of = iota((CHUNK, OWN), 0) // SLOT
        step_of = pos_of // 2
        owner_of = (zl - step_of + 4) % 4 * 8 + (xx + step_of - chunk + 8) % 4 * 2 + pos_of % 2
        spread = (owner_of == iota((CHUNK, OWN), 1)).astype(F32).astype(BF16)
        taken = mm(spread, place) == (iota((CHUNK, TOK), 0) % SLOT).astype(F32)
        weight_rows = mm(spread, w1) + mm(spread, w2) + mm(spread, w3)
        wsel = jnp.where(taken, weight_rows, 0.0)
        row_weight = jnp.sum(wsel, axis=1, keepdims=True)
        picks = jnp.where(taken, 1.0, 0.0).astype(BF16)
        sel16[lanes_of(chunk), :] = picks
        wsel_ref[lanes_of(chunk), :] = wsel
        x_rows = mm(picks, tok[...])
        c_rows = row_weight * mm(picks, cot[...])
        send[0, rows_of(chunk)] = x_rows.astype(BF16).reshape(BPC, SLOT, DQ)
        send[1, rows_of(chunk)] = c_rows.astype(BF16).reshape(BPC, SLOT, DQ)
        if first:
            pl.semaphore_wait(barrier, OWN - 1 + 5)

        @pl.loop(0, BPC)
        def _(step):
            dl, core2 = step // 2, step % 2
            other = (zl - dl + 4) % 4 * 8 + (xx + dl - chunk + 8) % 4 * 2 + core2
            src = send.at[:, chunk * BPC + step]
            dst = recv.at[:, chunk * BPC + dl * 2 + core]

            @pl.when(other == me)
            def _():
                pltpu.make_async_copy(src, dst, d_recv.at[chunk]).start()

            @pl.when(other != me)
            def _():
                remote(src, dst, d_send, d_recv.at[chunk], dev_own(other)).start()

    dispatch(across, first=True)
    dispatch(above)
    for load in loads[4:]:
        load.wait()

    def partials(chunk):
        block = recv.at[:, rows_of(chunk)]
        pltpu.make_async_copy(block, block, d_recv.at[chunk]).wait()
        x_rows = recv[0, rows_of(chunk)].reshape(CHUNK, DQ)
        c_rows = recv[1, rows_of(chunk)].reshape(CHUNK, DQ)
        return [mm(wgt[t], rows, (1, 1)) for t, rows in enumerate((x_rows, x_rows, c_rows))]

    def units(quarter):
        return pl.ds(*QUARTERS[quarter])

    devs = (dev_above, dev_below)
    copies = {}

    def go(kind, way, quarter, src, dst, sems):
        index = 4 * way + quarter
        copy = remote(src, dst, sems[0].at[index], sems[1].at[index], devs[way])
        copy.start()
        copies[kind, way, quarter] = copy

    def send_near(way, quarter):
        block = (way, slice(None), units(quarter))
        go("near", way, quarter, near.at[block], landed.at[block], (rs_send, rs_recv))

    for t, value in enumerate(partials(across)):
        far[t] = value.astype(BF16)
    for i in range(2):
        for way in (UP, DOWN):
            quarter = RELAYED[way][i]
            block = (slice(None), units(quarter))
            go("far", way, quarter, far.at[block], relay.at[block], (far_send, far_recv))
    for way, chunk, later in ((UP, above, below), (DOWN, below, aa)):
        dispatch(later)
        for t, value in enumerate(partials(chunk)):
            keep[way, t] = value
            near[way, t] = value.astype(BF16)
        send_near(way, RELAYED[1 - way][0])
    for i in range(2):
        for way in (UP, DOWN):
            quarter = RELAYED[way][i]
            copies["far", way, quarter].wait_recv()
            summed = keep[way, :, units(quarter)] + relay[:, units(quarter)].astype(F32)
            near[way, :, units(quarter)] = summed.astype(BF16)
            send_near(way, quarter)
        if i == 0:
            for way in (UP, DOWN):
                send_near(way, RELAYED[1 - way][1])
            for t, value in enumerate(partials(aa)):
                mine[t] = value

    wsel_t = wsel_ref[...].T
    hi = wsel_t.astype(BF16)
    whi_t[...] = hi
    wlo_t[...] = (wsel_t - hi.astype(F32)).astype(BF16)
    sel_t[...] = sel16[...].astype(F32).T.astype(BF16)

    def pass_on(kind, way, chunk, quarter, sems):
        block = hid.at[:, units(quarter), lanes_of(chunk)]
        go(kind, way, quarter, block, block, sems)

    def arrived(sems, way, chunk, quarter):
        block = hid.at[:, units(quarter), lanes_of(chunk)]
        pltpu.make_async_copy(block, block, sems.at[4 * way + quarter]).wait()

    for quarter in (0, 2, 1, 3):
        copies["near", UP, quarter].wait_recv()
        copies["near", DOWN, quarter].wait_recv()
        span = units(quarter)
        gating, up_proj, grad_hidden = [
            mine[t, span] + landed[UP, t, span].astype(F32) + landed[DOWN, t, span].astype(F32)
            for t in range(3)
        ]
        sigma = jax.nn.sigmoid(gating)
        grad_gate = grad_hidden * up_proj * sigma * (1.0 + gating * (1.0 - sigma))
        hid[0, span, lanes_of(aa)] = (gating * sigma * up_proj).astype(BF16)
        hid[1, span, lanes_of(aa)] = grad_gate.astype(BF16)
        hid[2, span, lanes_of(aa)] = (grad_hidden * gating * sigma).astype(BF16)
        first = UP if quarter in RELAYED[UP] else DOWN
        for way in (first, 1 - first):
            pass_on("own", way, aa, quarter, (ag_send, ag_recv))

    def give_back(chunk):
        lanes = lanes_of(chunk)
        out_rows = mm(hid[0, :, lanes], wgt[2], (0, 0))
        grad_rows = mm(hid[1, :, lanes], wgt[0], (0, 0)) + mm(hid[2, :, lanes], wgt[1], (0, 0))
        back[0, rows_of(chunk)] = out_rows.astype(BF16).reshape(BPC, SLOT, DQ)
        back[1, rows_of(chunk)] = grad_rows.astype(BF16).reshape(BPC, SLOT, DQ)

        @pl.loop(0, BPC)
        def _(step):
            dl, core2 = step // 2, step % 2
            other = (zl + dl) % 4 * 8 + (xx + chunk - dl + 4) % 4 * 2 + core2
            src = back.at[:, chunk * BPC + step]
            dst = home.at[:, chunk * BPC + dl * 2 + core]

            @pl.when(other == me)
            def _():
                pltpu.make_async_copy(src, dst, r_recv.at[chunk]).start()

            @pl.when(other != me)
            def _():
                remote(src, dst, r_send, r_recv.at[chunk], dev_own(other)).start()

    for i in range(2):
        for way, chunk in ((UP, below), (DOWN, above)):
            quarter = RELAYED[way][i]
            arrived(ag_recv, way, chunk, quarter)
            pass_on("on", way, chunk, quarter, (fw_send, fw_recv))
        if i == 0:
            give_back(aa)
    for way, chunk in ((UP, below), (DOWN, above)):
        for quarter in RELAYED[1 - way]:
            arrived(ag_recv, way, chunk, quarter)
        give_back(chunk)
    for way in (UP, DOWN):
        for quarter in RELAYED[way]:
            arrived(fw_recv, way, across, quarter)
    give_back(across)

    def arrived_home(chunk):
        block = home.at[:, rows_of(chunk)]
        pltpu.make_async_copy(block, block, r_recv.at[chunk]).wait()

    def combine(chunk, some=slice(None)):
        lanes = lanes_of(chunk)
        out_home = home[0, rows_of(chunk)].reshape(CHUNK, DQ)
        grad_home = home[1, rows_of(chunk)].reshape(CHUNK, DQ)
        return (
            mm(whi_t[some, lanes], out_home) + mm(wlo_t[some, lanes], out_home),
            mm(sel_t[some, lanes], grad_home),
        )

    arrived_home(aa)
    part[0], part[1] = combine(aa)
    for chunk in (below, above):
        arrived_home(chunk)
        layer, tgrad = combine(chunk)
        part[0] += layer
        part[1] += tgrad

    for side, kind, out in ((0, 1, gate_out), (0, 2, up_out), (1, 0, down_out)):
        out[...] = mm(hid[kind], recv[side].reshape(ROWS, DQ))

    kept = pl.ds(pl.multiple_of(cc * 256, 256), 256)
    given = pl.ds(pl.multiple_of((1 - cc) * 256, 256), 256)
    halves = (pl.ds(0, TOK // 2), pl.ds(TOK // 2, TOK // 2))
    arrived_home(across)
    cx = []
    for h, some in enumerate(halves):
        layer, tgrad = combine(across, some)
        part[0, some] += layer
        part[1, some] += tgrad
        cx_out[h] = part[:, some, given].astype(BF16)
        copy = remote(cx_out.at[h], cx_in.at[h], cx_send.at[h], cx_recv.at[h], dev_pair)
        copy.start()
        cx.append(copy)
    bx = []

    def hop_to(kind, h, src, dev):
        index = 3 * h + kind
        copy = remote(src, bx_in.at[kind, h], bx_send.at[index], bx_recv.at[index], dev)
        copy.start()
        bx.append(copy)

    for h, some in enumerate(halves):
        cx[h].wait_recv()
        total = part[:, some, kept] + cx_in[h].astype(F32)
        for p in range(4):
            piece = jnp.concatenate(
                [total[0, :, 64 * p : 64 * p + 64], total[1, :, 64 * p : 64 * p + 64]], axis=1
            )
            pieces[p, some] = piece
            bx_out[h, p] = piece.astype(BF16)
        far_dev, near_dev = (dev_b(1), dev_b(3)) if h == 0 else (dev_b(3), dev_b(1))
        near_b = (bb + 3) % 4 if h == 0 else (bb + 1) % 4
        hop_to(0, h, bx_out.at[h, (bb + 2) % 4], far_dev)
        hop_to(1, h, bx_out.at[h, near_b], near_dev)
    for h, some in enumerate(halves):
        bx[2 * h].wait_recv()
        far_dev = dev_b(1) if h == 0 else dev_b(3)
        far_b = (bb + 1) % 4 if h == 0 else (bb + 3) % 4
        bx_out[h, far_b] = (pieces[far_b, some] + bx_in[0, h].astype(F32)).astype(BF16)
        hop_to(2, h, bx_out.at[h, far_b], far_dev)
    for index in (1, 3, 4, 5):
        bx[index].wait_recv()
    final = jnp.concatenate(
        [
            pieces[bb, some] + bx_in[1, h].astype(F32) + bx_in[2, h].astype(F32)
            for h, some in enumerate(halves)
        ],
        axis=0,
    )
    final = final.T
    layer_ref[...] = final[:64].astype(BF16)
    tgrad_ref[...] = final[64:].astype(BF16)

    pltpu.make_async_copy(send.at[:, : OWN - 1], recv.at[:, : OWN - 1], d_send).wait()
    pltpu.make_async_copy(back.at[:, : OWN - 1], home.at[:, : OWN - 1], r_send).wait()
    for copy in list(copies.values()) + cx + bx:
        copy.wait_send()


def finish(*refs):
    given, out, held = refs[:5], refs[5:10], refs[10:15]
    in_sem, out_sem = refs[15:]
    loads = [pltpu.make_async_copy(given[i], held[i], in_sem.at[i]) for i in range(5)]
    stores = [pltpu.make_async_copy(held[i], out[i], out_sem.at[i]) for i in range(5)]
    for load in loads:
        load.start()
    for load, store in zip(loads, stores):
        load.wait()
        store.start()
    for store in stores:
        store.wait()


def on_device(tokens, cotangent, route_ids, route_weights, gate_weight, up_weight, down_weight_t):
    vmem = pl.BlockSpec(memory_space=pltpu.VMEM)
    hbm = pl.BlockSpec(memory_space=pl.ANY)
    dma = pltpu.SemaphoreType.DMA
    grad_shape = jax.ShapeDtypeStruct((FQ, DQ), F32)
    out_shape = jax.ShapeDtypeStruct((64, TOK), BF16)
    out_shapes = (out_shape, out_shape, grad_shape, grad_shape, grad_shape)
    results = pl.pallas_call(
        kernel,
        out_shape=out_shapes,
        in_specs=[hbm] * 7,
        out_specs=(vmem,) * 5,
        scratch_shapes=[
            pltpu.VMEM((TOP, TOK), jnp.int32),
            pltpu.VMEM((TOP, TOK), F32),
            pltpu.VMEM((TOK, DQ), BF16),
            pltpu.VMEM((TOK, DQ), BF16),
            pltpu.VMEM((3, FQ, DQ), BF16),
            pltpu.VMEM((ROWS, TOK), BF16),
            pltpu.VMEM((ROWS, TOK), F32),
            pltpu.VMEM((TOK, ROWS), BF16),
            pltpu.VMEM((TOK, ROWS), BF16),
            pltpu.VMEM((TOK, ROWS), BF16),
            pltpu.VMEM((2, OWN, SLOT, DQ), BF16),
            pltpu.VMEM((2, OWN, SLOT, DQ), BF16),
            pltpu.VMEM((3, FQ, CHUNK), BF16),
            pltpu.VMEM((3, FQ, CHUNK), BF16),
            pltpu.VMEM((2, 3, FQ, CHUNK), BF16),
            pltpu.VMEM((2, 3, FQ, CHUNK), F32),
            pltpu.VMEM((3, FQ, CHUNK), F32),
            pltpu.VMEM((2, 3, FQ, CHUNK), BF16),
            pltpu.VMEM((3, FQ, ROWS), BF16),
            pltpu.VMEM((2, OWN, SLOT, DQ), BF16),
            pltpu.VMEM((2, OWN, SLOT, DQ), BF16),
            pltpu.VMEM((2, TOK, DQ), F32),
            pltpu.VMEM((2, 2, TOK // 2, 256), BF16),
            pltpu.VMEM((2, 2, TOK // 2, 256), BF16),
            pltpu.VMEM((4, TOK, 128), F32),
            pltpu.VMEM((2, 4, TOK // 2, 128), BF16),
            pltpu.VMEM((3, 2, TOK // 2, 128), BF16),
            dma((7,)),
            dma,
            dma((4,)),
            dma((8,)),
            dma((8,)),
            dma((8,)),
            dma((8,)),
            dma((8,)),
            dma((8,)),
            dma((8,)),
            dma((8,)),
            dma,
            dma((4,)),
            dma((2,)),
            dma((2,)),
            dma((6,)),
            dma((6,)),
        ],
        compiler_params=pltpu.CompilerParams(
            collective_id=0, has_side_effects=True, vmem_limit_bytes=VMEM_LIMIT
        ),
        cost_estimate=pl.CostEstimate(
            flops=2 * 9 * ROWS * DQ * FQ, bytes_accessed=8 * 1024 * 1024, transcendentals=CHUNK * FQ
        ),
    )(
        route_ids.T,
        route_weights.T,
        tokens,
        cotangent,
        gate_weight[0].T,
        up_weight[0].T,
        down_weight_t[0].T,
    )
    layer_out, token_grad, gate_grad, up_grad, down_grad = pl.pallas_call(
        finish,
        out_shape=out_shapes,
        in_specs=[hbm] * 5,
        out_specs=(hbm,) * 5,
        scratch_shapes=[pltpu.VMEM(s.shape, s.dtype) for s in out_shapes] + [dma((5,)), dma((5,))],
        compiler_params=pltpu.CompilerParams(vmem_limit_bytes=VMEM_LIMIT),
        cost_estimate=pl.CostEstimate(
            flops=0, bytes_accessed=6 * DQ * FQ * 4, transcendentals=0
        ),
    )(*results)
    return (layer_out.T, token_grad.T, gate_grad.T[None], up_grad.T[None], down_grad.T[None])


def solution(mesh):
    placed = (
        P("own", None),
        P("own", None),
        P("own", None),
        P("own", None),
        P(("own", "grp"), None, None),
        P(("own", "grp"), None, None),
        P(("own", "grp"), None, None),
    )
    return jax.shard_map(
        on_device,
        mesh=mesh,
        in_specs=placed,
        out_specs=(
            P("own", "grp"),
            P("own", "grp"),
            P(("own", "grp"), None, None),
            P(("own", "grp"), None, None),
            P(("own", "grp"), None, None),
        ),
        check_vma=False,
    )
```

```python
import jax
import jax.numpy as jnp
from jax import lax
from jax.experimental import pallas as pl
from jax.experimental.pallas import tpu as pltpu
from jax.sharding import PartitionSpec as P

OWN = 32
SLOT = 16
TOK = 128
DQ = 512
FQ = 352
TOP = 6
ROWS = OWN * SLOT
BPC = 8
CHUNK = BPC * SLOT
QUARTERS = ((0, 96), (96, 80), (176, 96), (272, 80))
UP, DOWN = 0, 1
RELAYED = ((0, 1), (2, 3))
VMEM_LIMIT = 58 * 1024 * 1024
MESH = pl.DeviceIdType.MESH
F32 = jnp.float32
BF16 = jnp.bfloat16


def mm(lhs, rhs, contract=(1, 0)):
    return lax.dot_general(
        lhs,
        rhs,
        (((contract[0],), (contract[1],)), ((), ())),
        preferred_element_type=F32,
    )


def iota(shape, dim):
    return lax.broadcasted_iota(jnp.int32, shape, dim)


def kernel(
    ids_hbm,
    wts_hbm,
    tok_hbm,
    cot_hbm,
    gate_hbm,
    up_hbm,
    down_hbm,
    layer_ref,
    tgrad_ref,
    gate_out,
    up_out,
    down_out,
    ids_ref,
    wts_ref,
    tok,
    cot,
    wgt,
    sel16,
    wsel_ref,
    sel_t,
    whi_t,
    wlo_t,
    send,
    recv,
    far,
    relay,
    near,
    keep,
    mine,
    landed,
    hid,
    back,
    home,
    part,
    cx_out,
    cx_in,
    pieces,
    bx_out,
    bx_in,
    grads,
    in_sem,
    d_send,
    d_recv,
    far_send,
    far_recv,
    rs_send,
    rs_recv,
    ag_send,
    ag_recv,
    fw_send,
    fw_recv,
    r_send,
    r_recv,
    cx_send,
    cx_recv,
    bx_send,
    bx_recv,
    out_sem,
):
    me = lax.axis_index("own")
    grp = lax.axis_index("grp")
    zl, xx, core = me // 8, me % 8 // 2, me % 2
    yy, bb = grp // 4, grp % 4
    aa, cc = yy // 2, yy % 2
    zz = bb * 4 + zl
    above, below, across = (aa + 1) % 4, (aa + 3) % 4, (aa + 2) % 4
    dev_above = (me, (above * 2 + cc) * 4 + bb)
    dev_below = (me, (below * 2 + cc) * 4 + bb)
    dev_pair = (me, (aa * 2 + 1 - cc) * 4 + bb)

    def dev_own(other):
        zl2, core2 = other // 8, other % 2
        gap = (zl2 - zl + 4) % 4
        two = 2 - 4 * ((zl // 2 + core + core2) % 2)
        hop = jnp.where(gap == 2, two, jnp.where(gap == 3, -1, gap))
        return (other, yy * 4 + (zz + hop + 16) % 16 // 4)

    def dev_b(k):
        return (me, yy * 4 + (bb + k) % 4)

    def remote(src, dst, ssem, rsem, dev):
        return pltpu.make_async_remote_copy(
            src_ref=src,
            dst_ref=dst,
            send_sem=ssem,
            recv_sem=rsem,
            device_id=dev,
            device_id_type=MESH,
        )

    cols = pl.ds(pl.multiple_of(aa * DQ, DQ), DQ)
    loads = [
        pltpu.make_async_copy(ids_hbm, ids_ref, in_sem.at[5]),
        pltpu.make_async_copy(wts_hbm, wts_ref, in_sem.at[6]),
        pltpu.make_async_copy(tok_hbm.at[:, cols], tok, in_sem.at[0]),
        pltpu.make_async_copy(cot_hbm.at[:, cols], cot, in_sem.at[1]),
        pltpu.make_async_copy(gate_hbm, wgt.at[0], in_sem.at[2]),
        pltpu.make_async_copy(up_hbm, wgt.at[1], in_sem.at[3]),
        pltpu.make_async_copy(down_hbm, wgt.at[2], in_sem.at[4]),
    ]
    for load in loads:
        load.start()

    barrier = pltpu.get_barrier_semaphore()

    def greet(dev):
        pl.semaphore_signal(barrier, inc=1, device_id=dev, device_id_type=MESH)

    @pl.loop(1, OWN)
    def _(step):
        greet(dev_own((me + step) % OWN))

    for dev in (dev_above, dev_below, dev_pair, dev_b(1), dev_b(3)):
        greet(dev)

    loads[0].wait()
    loads[1].wait()
    expert = iota((OWN, TOK), 0) * 2 + cc
    named = jnp.zeros((OWN, TOK), F32)
    weight = jnp.zeros((OWN, TOK), F32)
    for k in range(TOP):
        hit = ids_ref[k : k + 1, :] == expert
        named = jnp.where(hit, 1.0, named)
        weight = jnp.where(hit, wts_ref[k : k + 1, :], weight)
    earlier = (iota((TOK, TOK), 0) < iota((TOK, TOK), 1)).astype(F32).astype(BF16)
    place = mm(named.astype(BF16), earlier)
    place = jnp.where(named > 0.5, place, -1.0).astype(BF16)
    w1 = weight.astype(BF16)
    rest = weight - w1.astype(F32)
    w2 = rest.astype(BF16)
    w3 = (rest - w2.astype(F32)).astype(BF16)
    for load in loads[2:4]:
        load.wait()

    def rows_of(chunk):
        return pl.ds(chunk * BPC, BPC)

    def lanes_of(chunk):
        return pl.ds(pl.multiple_of(chunk * CHUNK, CHUNK), CHUNK)

    def dispatch(chunk, first=False):
        pos_of = iota((CHUNK, OWN), 0) // SLOT
        step_of = pos_of // 2
        owner_of = (zl - step_of + 4) % 4 * 8 + (xx + step_of - chunk + 8) % 4 * 2 + pos_of % 2
        spread = (owner_of == iota((CHUNK, OWN), 1)).astype(F32).astype(BF16)
        taken = mm(spread, place) == (iota((CHUNK, TOK), 0) % SLOT).astype(F32)
        weight_rows = mm(spread, w1) + mm(spread, w2) + mm(spread, w3)
        wsel = jnp.where(taken, weight_rows, 0.0)
        row_weight = jnp.sum(wsel, axis=1, keepdims=True)
        picks = jnp.where(taken, 1.0, 0.0).astype(BF16)
        sel16[lanes_of(chunk), :] = picks
        wsel_ref[lanes_of(chunk), :] = wsel
        x_rows = mm(picks, tok[...])
        c_rows = row_weight * mm(picks, cot[...])
        send[0, rows_of(chunk)] = x_rows.astype(BF16).reshape(BPC, SLOT, DQ)
        send[1, rows_of(chunk)] = c_rows.astype(BF16).reshape(BPC, SLOT, DQ)
        if first:
            pl.semaphore_wait(barrier, OWN - 1 + 5)

        @pl.loop(0, BPC)
        def _(step):
            dl, core2 = step // 2, step % 2
            other = (zl - dl + 4) % 4 * 8 + (xx + dl - chunk + 8) % 4 * 2 + core2
            src = send.at[:, chunk * BPC + step]
            dst = recv.at[:, chunk * BPC + dl * 2 + core]

            @pl.when(other == me)
            def _():
                pltpu.make_async_copy(src, dst, d_recv.at[chunk]).start()

            @pl.when(other != me)
            def _():
                remote(src, dst, d_send, d_recv.at[chunk], dev_own(other)).start()

    dispatch(across, first=True)
    dispatch(above)
    for load in loads[4:]:
        load.wait()

    def partials(chunk):
        block = recv.at[:, rows_of(chunk)]
        pltpu.make_async_copy(block, block, d_recv.at[chunk]).wait()
        x_rows = recv[0, rows_of(chunk)].reshape(CHUNK, DQ)
        c_rows = recv[1, rows_of(chunk)].reshape(CHUNK, DQ)
        return [mm(wgt[t], rows, (1, 1)) for t, rows in enumerate((x_rows, x_rows, c_rows))]

    def units(quarter):
        return pl.ds(*QUARTERS[quarter])

    devs = (dev_above, dev_below)
    copies = {}

    def go(kind, way, quarter, src, dst, sems):
        index = 4 * way + quarter
        copy = remote(src, dst, sems[0].at[index], sems[1].at[index], devs[way])
        copy.start()
        copies[kind, way, quarter] = copy

    def send_near(way, quarter):
        block = (way, slice(None), units(quarter))
        go("near", way, quarter, near.at[block], landed.at[block], (rs_send, rs_recv))

    for t, value in enumerate(partials(across)):
        far[t] = value.astype(BF16)
    for i in range(2):
        for way in (UP, DOWN):
            quarter = RELAYED[way][i]
            block = (slice(None), units(quarter))
            go("far", way, quarter, far.at[block], relay.at[block], (far_send, far_recv))
    for way, chunk, later in ((UP, above, below), (DOWN, below, aa)):
        dispatch(later)
        for t, value in enumerate(partials(chunk)):
            keep[way, t] = value
            near[way, t] = value.astype(BF16)
        send_near(way, RELAYED[1 - way][0])
    for i in range(2):
        for way in (UP, DOWN):
            quarter = RELAYED[way][i]
            copies["far", way, quarter].wait_recv()
            summed = keep[way, :, units(quarter)] + relay[:, units(quarter)].astype(F32)
            near[way, :, units(quarter)] = summed.astype(BF16)
            send_near(way, quarter)
        if i == 0:
            for way in (UP, DOWN):
                send_near(way, RELAYED[1 - way][1])
            for t, value in enumerate(partials(aa)):
                mine[t] = value

    wsel_t = wsel_ref[...].T
    hi = wsel_t.astype(BF16)
    whi_t[...] = hi
    wlo_t[...] = (wsel_t - hi.astype(F32)).astype(BF16)
    sel_t[...] = sel16[...].astype(F32).T.astype(BF16)

    def pass_on(kind, way, chunk, quarter, sems):
        block = hid.at[:, units(quarter), lanes_of(chunk)]
        go(kind, way, quarter, block, block, sems)

    def arrived(sems, way, chunk, quarter):
        block = hid.at[:, units(quarter), lanes_of(chunk)]
        pltpu.make_async_copy(block, block, sems.at[4 * way + quarter]).wait()

    for quarter in (0, 2, 1, 3):
        copies["near", UP, quarter].wait_recv()
        copies["near", DOWN, quarter].wait_recv()
        span = units(quarter)
        gating, up_proj, grad_hidden = [
            mine[t, span] + landed[UP, t, span].astype(F32) + landed[DOWN, t, span].astype(F32)
            for t in range(3)
        ]
        sigma = jax.nn.sigmoid(gating)
        grad_gate = grad_hidden * up_proj * sigma * (1.0 + gating * (1.0 - sigma))
        hid[0, span, lanes_of(aa)] = (gating * sigma * up_proj).astype(BF16)
        hid[1, span, lanes_of(aa)] = grad_gate.astype(BF16)
        hid[2, span, lanes_of(aa)] = (grad_hidden * gating * sigma).astype(BF16)
        first = UP if quarter in RELAYED[UP] else DOWN
        for way in (first, 1 - first):
            pass_on("own", way, aa, quarter, (ag_send, ag_recv))

    def give_back(chunk):
        lanes = lanes_of(chunk)
        out_rows = mm(hid[0, :, lanes], wgt[2], (0, 0))
        grad_rows = mm(hid[1, :, lanes], wgt[0], (0, 0)) + mm(hid[2, :, lanes], wgt[1], (0, 0))
        back[0, rows_of(chunk)] = out_rows.astype(BF16).reshape(BPC, SLOT, DQ)
        back[1, rows_of(chunk)] = grad_rows.astype(BF16).reshape(BPC, SLOT, DQ)

        @pl.loop(0, BPC)
        def _(step):
            dl, core2 = step // 2, step % 2
            other = (zl + dl) % 4 * 8 + (xx + chunk - dl + 4) % 4 * 2 + core2
            src = back.at[:, chunk * BPC + step]
            dst = home.at[:, chunk * BPC + dl * 2 + core]

            @pl.when(other == me)
            def _():
                pltpu.make_async_copy(src, dst, r_recv.at[chunk]).start()

            @pl.when(other != me)
            def _():
                remote(src, dst, r_send, r_recv.at[chunk], dev_own(other)).start()

    for i in range(2):
        for way, chunk in ((UP, below), (DOWN, above)):
            quarter = RELAYED[way][i]
            arrived(ag_recv, way, chunk, quarter)
            pass_on("on", way, chunk, quarter, (fw_send, fw_recv))
        if i == 0:
            give_back(aa)
    for way, chunk in ((UP, below), (DOWN, above)):
        for quarter in RELAYED[1 - way]:
            arrived(ag_recv, way, chunk, quarter)
        give_back(chunk)
    for way in (UP, DOWN):
        for quarter in RELAYED[way]:
            arrived(fw_recv, way, across, quarter)
    give_back(across)

    def arrived_home(chunk):
        block = home.at[:, rows_of(chunk)]
        pltpu.make_async_copy(block, block, r_recv.at[chunk]).wait()

    def combine(chunk, some=slice(None)):
        lanes = lanes_of(chunk)
        out_home = home[0, rows_of(chunk)].reshape(CHUNK, DQ)
        grad_home = home[1, rows_of(chunk)].reshape(CHUNK, DQ)
        return (
            mm(whi_t[some, lanes], out_home) + mm(wlo_t[some, lanes], out_home),
            mm(sel_t[some, lanes], grad_home),
        )

    arrived_home(aa)
    part[0], part[1] = combine(aa)
    for chunk in (below, above):
        arrived_home(chunk)
        layer, tgrad = combine(chunk)
        part[0] += layer
        part[1] += tgrad

    stores = []
    for t, (side, kind, out) in enumerate(((0, 1, gate_out), (0, 2, up_out), (1, 0, down_out))):
        grads[t] = mm(hid[kind], recv[side].reshape(ROWS, DQ))
        store = pltpu.make_async_copy(grads.at[t], out, out_sem.at[t])
        store.start()
        stores.append(store)

    kept = pl.ds(pl.multiple_of(cc * 256, 256), 256)
    given = pl.ds(pl.multiple_of((1 - cc) * 256, 256), 256)
    halves = (pl.ds(0, TOK // 2), pl.ds(TOK // 2, TOK // 2))
    arrived_home(across)
    cx = []
    for h, some in enumerate(halves):
        layer, tgrad = combine(across, some)
        part[0, some] += layer
        part[1, some] += tgrad
        cx_out[h] = part[:, some, given].astype(BF16)
        copy = remote(cx_out.at[h], cx_in.at[h], cx_send.at[h], cx_recv.at[h], dev_pair)
        copy.start()
        cx.append(copy)
    bx = []

    def hop_to(kind, h, src, dev):
        index = 3 * h + kind
        copy = remote(src, bx_in.at[kind, h], bx_send.at[index], bx_recv.at[index], dev)
        copy.start()
        bx.append(copy)

    for h, some in enumerate(halves):
        cx[h].wait_recv()
        total = part[:, some, kept] + cx_in[h].astype(F32)
        for p in range(4):
            piece = jnp.concatenate(
                [total[0, :, 64 * p : 64 * p + 64], total[1, :, 64 * p : 64 * p + 64]], axis=1
            )
            pieces[p, some] = piece
            bx_out[h, p] = piece.astype(BF16)
        far_dev, near_dev = (dev_b(1), dev_b(3)) if h == 0 else (dev_b(3), dev_b(1))
        near_b = (bb + 3) % 4 if h == 0 else (bb + 1) % 4
        hop_to(0, h, bx_out.at[h, (bb + 2) % 4], far_dev)
        hop_to(1, h, bx_out.at[h, near_b], near_dev)
    for h, some in enumerate(halves):
        bx[2 * h].wait_recv()
        far_dev = dev_b(1) if h == 0 else dev_b(3)
        far_b = (bb + 1) % 4 if h == 0 else (bb + 3) % 4
        bx_out[h, far_b] = (pieces[far_b, some] + bx_in[0, h].astype(F32)).astype(BF16)
        hop_to(2, h, bx_out.at[h, far_b], far_dev)
    for index in (1, 3, 4, 5):
        bx[index].wait_recv()
    final = jnp.concatenate(
        [
            pieces[bb, some] + bx_in[1, h].astype(F32) + bx_in[2, h].astype(F32)
            for h, some in enumerate(halves)
        ],
        axis=0,
    )
    final = final.T
    layer_ref[...] = final[:64].astype(BF16)
    tgrad_ref[...] = final[64:].astype(BF16)

    pltpu.make_async_copy(send.at[:, : OWN - 1], recv.at[:, : OWN - 1], d_send).wait()
    pltpu.make_async_copy(back.at[:, : OWN - 1], home.at[:, : OWN - 1], r_send).wait()
    for copy in list(copies.values()) + cx + bx:
        copy.wait_send()
    for store in stores:
        store.wait()


def finish(*refs):
    given, out, held = refs[:5], refs[5:10], refs[10:15]
    in_sem, out_sem = refs[15:]
    loads = [pltpu.make_async_copy(given[i], held[i], in_sem.at[i]) for i in range(5)]
    stores = [pltpu.make_async_copy(held[i], out[i], out_sem.at[i]) for i in range(5)]
    for load in loads:
        load.start()
    for load, store in zip(loads, stores):
        load.wait()
        store.start()
    for store in stores:
        store.wait()


def on_device(tokens, cotangent, route_ids, route_weights, gate_weight, up_weight, down_weight_t):
    vmem = pl.BlockSpec(memory_space=pltpu.VMEM)
    hbm = pl.BlockSpec(memory_space=pl.ANY)
    dma = pltpu.SemaphoreType.DMA
    grad_shape = jax.ShapeDtypeStruct((FQ, DQ), F32)
    out_shape = jax.ShapeDtypeStruct((64, TOK), BF16)
    out_shapes = (out_shape, out_shape, grad_shape, grad_shape, grad_shape)
    results = pl.pallas_call(
        kernel,
        out_shape=out_shapes,
        in_specs=[hbm] * 7,
        out_specs=(vmem, vmem, hbm, hbm, hbm),
        scratch_shapes=[
            pltpu.VMEM((TOP, TOK), jnp.int32),
            pltpu.VMEM((TOP, TOK), F32),
            pltpu.VMEM((TOK, DQ), BF16),
            pltpu.VMEM((TOK, DQ), BF16),
            pltpu.VMEM((3, FQ, DQ), BF16),
            pltpu.VMEM((ROWS, TOK), BF16),
            pltpu.VMEM((ROWS, TOK), F32),
            pltpu.VMEM((TOK, ROWS), BF16),
            pltpu.VMEM((TOK, ROWS), BF16),
            pltpu.VMEM((TOK, ROWS), BF16),
            pltpu.VMEM((2, OWN, SLOT, DQ), BF16),
            pltpu.VMEM((2, OWN, SLOT, DQ), BF16),
            pltpu.VMEM((3, FQ, CHUNK), BF16),
            pltpu.VMEM((3, FQ, CHUNK), BF16),
            pltpu.VMEM((2, 3, FQ, CHUNK), BF16),
            pltpu.VMEM((2, 3, FQ, CHUNK), F32),
            pltpu.VMEM((3, FQ, CHUNK), F32),
            pltpu.VMEM((2, 3, FQ, CHUNK), BF16),
            pltpu.VMEM((3, FQ, ROWS), BF16),
            pltpu.VMEM((2, OWN, SLOT, DQ), BF16),
            pltpu.VMEM((2, OWN, SLOT, DQ), BF16),
            pltpu.VMEM((2, TOK, DQ), F32),
            pltpu.VMEM((2, 2, TOK // 2, 256), BF16),
            pltpu.VMEM((2, 2, TOK // 2, 256), BF16),
            pltpu.VMEM((4, TOK, 128), F32),
            pltpu.VMEM((2, 4, TOK // 2, 128), BF16),
            pltpu.VMEM((3, 2, TOK // 2, 128), BF16),
            pltpu.VMEM((3, FQ, DQ), F32),
            dma((7,)),
            dma,
            dma((4,)),
            dma((8,)),
            dma((8,)),
            dma((8,)),
            dma((8,)),
            dma((8,)),
            dma((8,)),
            dma((8,)),
            dma((8,)),
            dma,
            dma((4,)),
            dma((2,)),
            dma((2,)),
            dma((6,)),
            dma((6,)),
            dma((3,)),
        ],
        compiler_params=pltpu.CompilerParams(
            collective_id=0, has_side_effects=True, vmem_limit_bytes=VMEM_LIMIT
        ),
        cost_estimate=pl.CostEstimate(
            flops=2 * 9 * ROWS * DQ * FQ, bytes_accessed=8 * 1024 * 1024, transcendentals=CHUNK * FQ
        ),
    )(
        route_ids.T,
        route_weights.T,
        tokens,
        cotangent,
        gate_weight[0].T,
        up_weight[0].T,
        down_weight_t[0].T,
    )
    layer_out, token_grad, gate_grad, up_grad, down_grad = pl.pallas_call(
        finish,
        out_shape=out_shapes,
        in_specs=[hbm] * 5,
        out_specs=(hbm,) * 5,
        scratch_shapes=[pltpu.VMEM(s.shape, s.dtype) for s in out_shapes] + [dma((5,)), dma((5,))],
        compiler_params=pltpu.CompilerParams(vmem_limit_bytes=VMEM_LIMIT),
        cost_estimate=pl.CostEstimate(
            flops=0, bytes_accessed=6 * DQ * FQ * 4, transcendentals=0
        ),
    )(*results)
    return (layer_out.T, token_grad.T, gate_grad.T[None], up_grad.T[None], down_grad.T[None])


def solution(mesh):
    placed = (
        P("own", None),
        P("own", None),
        P("own", None),
        P("own", None),
        P(("own", "grp"), None, None),
        P(("own", "grp"), None, None),
        P(("own", "grp"), None, None),
    )
    return jax.shard_map(
        on_device,
        mesh=mesh,
        in_specs=placed,
        out_specs=(
            P("own", "grp"),
            P("own", "grp"),
            P(("own", "grp"), None, None),
            P(("own", "grp"), None, None),
            P(("own", "grp"), None, None),
        ),
        check_vma=False,
    )
```

```python
import jax
import jax.numpy as jnp
from jax import lax
from jax.experimental import pallas as pl
from jax.experimental.pallas import tpu as pltpu
from jax.sharding import PartitionSpec as P

OWN = 32
SLOT = 16
TOK = 128
DQ = 512
FQ = 352
TOP = 6
ROWS = OWN * SLOT
BPC = 8
CHUNK = BPC * SLOT
QUARTERS = ((0, 96), (96, 80), (176, 96), (272, 80))
UP, DOWN = 0, 1
RELAYED = ((0, 1), (2, 3))
VMEM_LIMIT = 58 * 1024 * 1024
MESH = pl.DeviceIdType.MESH
F32 = jnp.float32
BF16 = jnp.bfloat16


def mm(lhs, rhs, contract=(1, 0)):
    return lax.dot_general(
        lhs,
        rhs,
        (((contract[0],), (contract[1],)), ((), ())),
        preferred_element_type=F32,
    )


def iota(shape, dim):
    return lax.broadcasted_iota(jnp.int32, shape, dim)


def kernel(
    ids_hbm,
    wts_hbm,
    tok_hbm,
    cot_hbm,
    gate_hbm,
    up_hbm,
    down_hbm,
    layer_ref,
    tgrad_ref,
    gate_out,
    up_out,
    down_out,
    ids_ref,
    wts_ref,
    tok,
    cot,
    wgt,
    sel16,
    wsel_ref,
    sel_t,
    whi_t,
    wlo_t,
    send,
    recv,
    far,
    relay,
    near,
    keep,
    mine,
    landed,
    hid,
    back,
    home,
    part,
    cx_out,
    cx_in,
    pieces,
    bx_out,
    bx_in,
    grads,
    in_sem,
    d_send,
    d_recv,
    far_send,
    far_recv,
    rs_send,
    rs_recv,
    ag_send,
    ag_recv,
    fw_send,
    fw_recv,
    r_send,
    r_recv,
    cx_send,
    cx_recv,
    bx_send,
    bx_recv,
    out_sem,
):
    me = lax.axis_index("own")
    grp = lax.axis_index("grp")
    zl, xx, core = me // 8, me % 8 // 2, me % 2
    yy, bb = grp // 4, grp % 4
    aa, cc = yy // 2, yy % 2
    zz = bb * 4 + zl
    above, below, across = (aa + 1) % 4, (aa + 3) % 4, (aa + 2) % 4
    dev_above = (me, (above * 2 + cc) * 4 + bb)
    dev_below = (me, (below * 2 + cc) * 4 + bb)
    dev_pair = (me, (aa * 2 + 1 - cc) * 4 + bb)

    def dev_own(other):
        zl2, core2 = other // 8, other % 2
        gap = (zl2 - zl + 4) % 4
        two = 2 - 4 * ((zl // 2 + core + core2) % 2)
        hop = jnp.where(gap == 2, two, jnp.where(gap == 3, -1, gap))
        return (other, yy * 4 + (zz + hop + 16) % 16 // 4)

    def dev_b(k):
        return (me, yy * 4 + (bb + k) % 4)

    def remote(src, dst, ssem, rsem, dev):
        return pltpu.make_async_remote_copy(
            src_ref=src,
            dst_ref=dst,
            send_sem=ssem,
            recv_sem=rsem,
            device_id=dev,
            device_id_type=MESH,
        )

    cols = pl.ds(pl.multiple_of(aa * DQ, DQ), DQ)
    loads = [
        pltpu.make_async_copy(ids_hbm, ids_ref, in_sem.at[5]),
        pltpu.make_async_copy(wts_hbm, wts_ref, in_sem.at[6]),
        pltpu.make_async_copy(tok_hbm.at[:, cols], tok, in_sem.at[0]),
        pltpu.make_async_copy(cot_hbm.at[:, cols], cot, in_sem.at[1]),
        pltpu.make_async_copy(gate_hbm, wgt.at[0], in_sem.at[2]),
        pltpu.make_async_copy(up_hbm, wgt.at[1], in_sem.at[3]),
        pltpu.make_async_copy(down_hbm, wgt.at[2], in_sem.at[4]),
    ]
    for load in loads:
        load.start()

    barrier = pltpu.get_barrier_semaphore()

    def greet(dev):
        pl.semaphore_signal(barrier, inc=1, device_id=dev, device_id_type=MESH)

    @pl.loop(1, OWN)
    def _(step):
        greet(dev_own((me + step) % OWN))

    for dev in (dev_above, dev_below, dev_pair, dev_b(1), dev_b(3)):
        greet(dev)

    loads[0].wait()
    loads[1].wait()
    expert = iota((OWN, TOK), 0) * 2 + cc
    named = jnp.zeros((OWN, TOK), F32)
    weight = jnp.zeros((OWN, TOK), F32)
    for k in range(TOP):
        hit = ids_ref[k : k + 1, :] == expert
        named = jnp.where(hit, 1.0, named)
        weight = jnp.where(hit, wts_ref[k : k + 1, :], weight)
    earlier = (iota((TOK, TOK), 0) < iota((TOK, TOK), 1)).astype(F32).astype(BF16)
    place = mm(named.astype(BF16), earlier)
    place = jnp.where(named > 0.5, place, -1.0).astype(BF16)
    w1 = weight.astype(BF16)
    rest = weight - w1.astype(F32)
    w2 = rest.astype(BF16)
    w3 = (rest - w2.astype(F32)).astype(BF16)
    for load in loads[2:4]:
        load.wait()

    def rows_of(chunk):
        return pl.ds(chunk * BPC, BPC)

    def lanes_of(chunk):
        return pl.ds(pl.multiple_of(chunk * CHUNK, CHUNK), CHUNK)

    def select(chunk):
        pos_of = iota((CHUNK, OWN), 0) // SLOT
        step_of = pos_of // 2
        owner_of = (zl - step_of + 4) % 4 * 8 + (xx + step_of - chunk + 8) % 4 * 2 + pos_of % 2
        spread = (owner_of == iota((CHUNK, OWN), 1)).astype(F32).astype(BF16)
        taken = mm(spread, place) == (iota((CHUNK, TOK), 0) % SLOT).astype(F32)
        weight_rows = mm(spread, w1) + mm(spread, w2) + mm(spread, w3)
        wsel = jnp.where(taken, weight_rows, 0.0)
        row_weight = jnp.sum(wsel, axis=1, keepdims=True)
        picks = jnp.where(taken, 1.0, 0.0).astype(BF16)
        sel16[lanes_of(chunk), :] = picks
        wsel_ref[lanes_of(chunk), :] = wsel
        x_rows = mm(picks, tok[...])
        c_rows = row_weight * mm(picks, cot[...])
        send[0, rows_of(chunk)] = x_rows.astype(BF16).reshape(BPC, SLOT, DQ)
        send[1, rows_of(chunk)] = c_rows.astype(BF16).reshape(BPC, SLOT, DQ)

    def dispatch(chunk):
        @pl.loop(0, BPC)
        def _(step):
            dl, core2 = step // 2, step % 2
            other = (zl - dl + 4) % 4 * 8 + (xx + dl - chunk + 8) % 4 * 2 + core2
            src = send.at[:, chunk * BPC + step]
            dst = recv.at[:, chunk * BPC + dl * 2 + core]

            @pl.when(other == me)
            def _():
                pltpu.make_async_copy(src, dst, d_recv.at[chunk]).start()

            @pl.when(other != me)
            def _():
                remote(src, dst, d_send, d_recv.at[chunk], dev_own(other)).start()

    select(across)
    pl.semaphore_wait(barrier, OWN - 1 + 5)
    dispatch(across)
    select(above)
    dispatch(above)
    select(below)
    select(aa)
    for load in loads[4:]:
        load.wait()

    def partials(chunk):
        block = recv.at[:, rows_of(chunk)]
        pltpu.make_async_copy(block, block, d_recv.at[chunk]).wait()
        x_rows = recv[0, rows_of(chunk)].reshape(CHUNK, DQ)
        c_rows = recv[1, rows_of(chunk)].reshape(CHUNK, DQ)
        return [mm(wgt[t], rows, (1, 1)) for t, rows in enumerate((x_rows, x_rows, c_rows))]

    def units(quarter):
        return pl.ds(*QUARTERS[quarter])

    devs = (dev_above, dev_below)
    copies = {}

    def go(kind, way, quarter, src, dst, sems):
        index = 4 * way + quarter
        copy = remote(src, dst, sems[0].at[index], sems[1].at[index], devs[way])
        copy.start()
        copies[kind, way, quarter] = copy

    def send_near(way, quarter):
        block = (way, slice(None), units(quarter))
        go("near", way, quarter, near.at[block], landed.at[block], (rs_send, rs_recv))

    for t, value in enumerate(partials(across)):
        far[t] = value.astype(BF16)
    for i in range(2):
        for way in (UP, DOWN):
            quarter = RELAYED[way][i]
            block = (slice(None), units(quarter))
            go("far", way, quarter, far.at[block], relay.at[block], (far_send, far_recv))
    for way, chunk, later in ((UP, above, below), (DOWN, below, aa)):
        dispatch(later)
        for t, value in enumerate(partials(chunk)):
            keep[way, t] = value
            near[way, t] = value.astype(BF16)
        send_near(way, RELAYED[1 - way][0])
    for i in range(2):
        for way in (UP, DOWN):
            quarter = RELAYED[way][i]
            copies["far", way, quarter].wait_recv()
            summed = keep[way, :, units(quarter)] + relay[:, units(quarter)].astype(F32)
            near[way, :, units(quarter)] = summed.astype(BF16)
            send_near(way, quarter)
        if i == 0:
            for way in (UP, DOWN):
                send_near(way, RELAYED[1 - way][1])
            for t, value in enumerate(partials(aa)):
                mine[t] = value

    wsel_t = wsel_ref[...].T
    hi = wsel_t.astype(BF16)
    whi_t[...] = hi
    wlo_t[...] = (wsel_t - hi.astype(F32)).astype(BF16)
    sel_t[...] = sel16[...].astype(F32).T.astype(BF16)

    def pass_on(kind, way, chunk, quarter, sems):
        block = hid.at[:, units(quarter), lanes_of(chunk)]
        go(kind, way, quarter, block, block, sems)

    def arrived(sems, way, chunk, quarter):
        block = hid.at[:, units(quarter), lanes_of(chunk)]
        pltpu.make_async_copy(block, block, sems.at[4 * way + quarter]).wait()

    for quarter in (0, 2, 1, 3):
        copies["near", UP, quarter].wait_recv()
        copies["near", DOWN, quarter].wait_recv()
        span = units(quarter)
        gating, up_proj, grad_hidden = [
            mine[t, span] + landed[UP, t, span].astype(F32) + landed[DOWN, t, span].astype(F32)
            for t in range(3)
        ]
        sigma = jax.nn.sigmoid(gating)
        grad_gate = grad_hidden * up_proj * sigma * (1.0 + gating * (1.0 - sigma))
        hid[0, span, lanes_of(aa)] = (gating * sigma * up_proj).astype(BF16)
        hid[1, span, lanes_of(aa)] = grad_gate.astype(BF16)
        hid[2, span, lanes_of(aa)] = (grad_hidden * gating * sigma).astype(BF16)
        first = UP if quarter in RELAYED[UP] else DOWN
        for way in (first, 1 - first):
            pass_on("own", way, aa, quarter, (ag_send, ag_recv))

    def give_back(chunk):
        lanes = lanes_of(chunk)
        out_rows = mm(hid[0, :, lanes], wgt[2], (0, 0))
        grad_rows = mm(hid[1, :, lanes], wgt[0], (0, 0)) + mm(hid[2, :, lanes], wgt[1], (0, 0))
        back[0, rows_of(chunk)] = out_rows.astype(BF16).reshape(BPC, SLOT, DQ)
        back[1, rows_of(chunk)] = grad_rows.astype(BF16).reshape(BPC, SLOT, DQ)

        @pl.loop(0, BPC)
        def _(step):
            dl, core2 = step // 2, step % 2
            other = (zl + dl) % 4 * 8 + (xx + chunk - dl + 4) % 4 * 2 + core2
            src = back.at[:, chunk * BPC + step]
            dst = home.at[:, chunk * BPC + dl * 2 + core]

            @pl.when(other == me)
            def _():
                pltpu.make_async_copy(src, dst, r_recv.at[chunk]).start()

            @pl.when(other != me)
            def _():
                remote(src, dst, r_send, r_recv.at[chunk], dev_own(other)).start()

    for i in range(2):
        for way, chunk in ((UP, below), (DOWN, above)):
            quarter = RELAYED[way][i]
            arrived(ag_recv, way, chunk, quarter)
            pass_on("on", way, chunk, quarter, (fw_send, fw_recv))
        if i == 0:
            give_back(aa)
    for way, chunk in ((UP, below), (DOWN, above)):
        for quarter in RELAYED[1 - way]:
            arrived(ag_recv, way, chunk, quarter)
        give_back(chunk)
    for way in (UP, DOWN):
        for quarter in RELAYED[way]:
            arrived(fw_recv, way, across, quarter)
    give_back(across)

    def arrived_home(chunk):
        block = home.at[:, rows_of(chunk)]
        pltpu.make_async_copy(block, block, r_recv.at[chunk]).wait()

    def combine(chunk, some=slice(None)):
        lanes = lanes_of(chunk)
        out_home = home[0, rows_of(chunk)].reshape(CHUNK, DQ)
        grad_home = home[1, rows_of(chunk)].reshape(CHUNK, DQ)
        return (
            mm(whi_t[some, lanes], out_home) + mm(wlo_t[some, lanes], out_home),
            mm(sel_t[some, lanes], grad_home),
        )

    arrived_home(aa)
    part[0], part[1] = combine(aa)
    for chunk in (below, above):
        arrived_home(chunk)
        layer, tgrad = combine(chunk)
        part[0] += layer
        part[1] += tgrad

    stores = []
    for t, (side, kind, out) in enumerate(((0, 1, gate_out), (0, 2, up_out), (1, 0, down_out))):
        grads[t] = mm(hid[kind], recv[side].reshape(ROWS, DQ))
        store = pltpu.make_async_copy(grads.at[t], out, out_sem.at[t])
        store.start()
        stores.append(store)

    kept = pl.ds(pl.multiple_of(cc * 256, 256), 256)
    given = pl.ds(pl.multiple_of((1 - cc) * 256, 256), 256)
    halves = (pl.ds(0, TOK // 2), pl.ds(TOK // 2, TOK // 2))
    arrived_home(across)
    cx = []
    for h, some in enumerate(halves):
        layer, tgrad = combine(across, some)
        part[0, some] += layer
        part[1, some] += tgrad
        cx_out[h] = part[:, some, given].astype(BF16)
        copy = remote(cx_out.at[h], cx_in.at[h], cx_send.at[h], cx_recv.at[h], dev_pair)
        copy.start()
        cx.append(copy)
    bx = []

    def hop_to(kind, h, src, dev):
        index = 3 * h + kind
        copy = remote(src, bx_in.at[kind, h], bx_send.at[index], bx_recv.at[index], dev)
        copy.start()
        bx.append(copy)

    for h, some in enumerate(halves):
        cx[h].wait_recv()
        total = part[:, some, kept] + cx_in[h].astype(F32)
        for p in range(4):
            piece = jnp.concatenate(
                [total[0, :, 64 * p : 64 * p + 64], total[1, :, 64 * p : 64 * p + 64]], axis=1
            )
            pieces[p, some] = piece
            bx_out[h, p] = piece.astype(BF16)
        far_dev, near_dev = (dev_b(1), dev_b(3)) if h == 0 else (dev_b(3), dev_b(1))
        near_b = (bb + 3) % 4 if h == 0 else (bb + 1) % 4
        hop_to(0, h, bx_out.at[h, (bb + 2) % 4], far_dev)
        hop_to(1, h, bx_out.at[h, near_b], near_dev)
    for h, some in enumerate(halves):
        bx[2 * h].wait_recv()
        far_dev = dev_b(1) if h == 0 else dev_b(3)
        far_b = (bb + 1) % 4 if h == 0 else (bb + 3) % 4
        bx_out[h, far_b] = (pieces[far_b, some] + bx_in[0, h].astype(F32)).astype(BF16)
        hop_to(2, h, bx_out.at[h, far_b], far_dev)
    for index in (1, 3, 4, 5):
        bx[index].wait_recv()
    final = jnp.concatenate(
        [
            pieces[bb, some] + bx_in[1, h].astype(F32) + bx_in[2, h].astype(F32)
            for h, some in enumerate(halves)
        ],
        axis=0,
    )
    final = final.T
    layer_ref[...] = final[:64].astype(BF16)
    tgrad_ref[...] = final[64:].astype(BF16)

    pltpu.make_async_copy(send.at[:, : OWN - 1], recv.at[:, : OWN - 1], d_send).wait()
    pltpu.make_async_copy(back.at[:, : OWN - 1], home.at[:, : OWN - 1], r_send).wait()
    for copy in list(copies.values()) + cx + bx:
        copy.wait_send()
    for store in stores:
        store.wait()


def finish(*refs):
    given, out, held = refs[:5], refs[5:10], refs[10:15]
    in_sem, out_sem = refs[15:]
    loads = [pltpu.make_async_copy(given[i], held[i], in_sem.at[i]) for i in range(5)]
    stores = [pltpu.make_async_copy(held[i], out[i], out_sem.at[i]) for i in range(5)]
    for load in loads:
        load.start()
    for load, store in zip(loads, stores):
        load.wait()
        store.start()
    for store in stores:
        store.wait()


def on_device(tokens, cotangent, route_ids, route_weights, gate_weight, up_weight, down_weight_t):
    vmem = pl.BlockSpec(memory_space=pltpu.VMEM)
    hbm = pl.BlockSpec(memory_space=pl.ANY)
    dma = pltpu.SemaphoreType.DMA
    grad_shape = jax.ShapeDtypeStruct((FQ, DQ), F32)
    out_shape = jax.ShapeDtypeStruct((64, TOK), BF16)
    out_shapes = (out_shape, out_shape, grad_shape, grad_shape, grad_shape)
    results = pl.pallas_call(
        kernel,
        out_shape=out_shapes,
        in_specs=[hbm] * 7,
        out_specs=(vmem, vmem, hbm, hbm, hbm),
        scratch_shapes=[
            pltpu.VMEM((TOP, TOK), jnp.int32),
            pltpu.VMEM((TOP, TOK), F32),
            pltpu.VMEM((TOK, DQ), BF16),
            pltpu.VMEM((TOK, DQ), BF16),
            pltpu.VMEM((3, FQ, DQ), BF16),
            pltpu.VMEM((ROWS, TOK), BF16),
            pltpu.VMEM((ROWS, TOK), F32),
            pltpu.VMEM((TOK, ROWS), BF16),
            pltpu.VMEM((TOK, ROWS), BF16),
            pltpu.VMEM((TOK, ROWS), BF16),
            pltpu.VMEM((2, OWN, SLOT, DQ), BF16),
            pltpu.VMEM((2, OWN, SLOT, DQ), BF16),
            pltpu.VMEM((3, FQ, CHUNK), BF16),
            pltpu.VMEM((3, FQ, CHUNK), BF16),
            pltpu.VMEM((2, 3, FQ, CHUNK), BF16),
            pltpu.VMEM((2, 3, FQ, CHUNK), F32),
            pltpu.VMEM((3, FQ, CHUNK), F32),
            pltpu.VMEM((2, 3, FQ, CHUNK), BF16),
            pltpu.VMEM((3, FQ, ROWS), BF16),
            pltpu.VMEM((2, OWN, SLOT, DQ), BF16),
            pltpu.VMEM((2, OWN, SLOT, DQ), BF16),
            pltpu.VMEM((2, TOK, DQ), F32),
            pltpu.VMEM((2, 2, TOK // 2, 256), BF16),
            pltpu.VMEM((2, 2, TOK // 2, 256), BF16),
            pltpu.VMEM((4, TOK, 128), F32),
            pltpu.VMEM((2, 4, TOK // 2, 128), BF16),
            pltpu.VMEM((3, 2, TOK // 2, 128), BF16),
            pltpu.VMEM((3, FQ, DQ), F32),
            dma((7,)),
            dma,
            dma((4,)),
            dma((8,)),
            dma((8,)),
            dma((8,)),
            dma((8,)),
            dma((8,)),
            dma((8,)),
            dma((8,)),
            dma((8,)),
            dma,
            dma((4,)),
            dma((2,)),
            dma((2,)),
            dma((6,)),
            dma((6,)),
            dma((3,)),
        ],
        compiler_params=pltpu.CompilerParams(
            collective_id=0, has_side_effects=True, vmem_limit_bytes=VMEM_LIMIT
        ),
        cost_estimate=pl.CostEstimate(
            flops=2 * 9 * ROWS * DQ * FQ, bytes_accessed=8 * 1024 * 1024, transcendentals=CHUNK * FQ
        ),
    )(
        route_ids.T,
        route_weights.T,
        tokens,
        cotangent,
        gate_weight[0].T,
        up_weight[0].T,
        down_weight_t[0].T,
    )
    layer_out, token_grad, gate_grad, up_grad, down_grad = pl.pallas_call(
        finish,
        out_shape=out_shapes,
        in_specs=[hbm] * 5,
        out_specs=(hbm,) * 5,
        scratch_shapes=[pltpu.VMEM(s.shape, s.dtype) for s in out_shapes] + [dma((5,)), dma((5,))],
        compiler_params=pltpu.CompilerParams(vmem_limit_bytes=VMEM_LIMIT),
        cost_estimate=pl.CostEstimate(
            flops=0, bytes_accessed=6 * DQ * FQ * 4, transcendentals=0
        ),
    )(*results)
    return (layer_out.T, token_grad.T, gate_grad.T[None], up_grad.T[None], down_grad.T[None])


def solution(mesh):
    placed = (
        P("own", None),
        P("own", None),
        P("own", None),
        P("own", None),
        P(("own", "grp"), None, None),
        P(("own", "grp"), None, None),
        P(("own", "grp"), None, None),
    )
    return jax.shard_map(
        on_device,
        mesh=mesh,
        in_specs=placed,
        out_specs=(
            P("own", "grp"),
            P("own", "grp"),
            P(("own", "grp"), None, None),
            P(("own", "grp"), None, None),
            P(("own", "grp"), None, None),
        ),
        check_vma=False,
    )
```
